256 devices in a mesh: grp: 8 (over y, core), seq: 32 (over x, z).
Axes of the slice: x: 4, y: 4, z: 8, core: 2. Of those that a mesh axis runs over, the one named last changes fastest.
Arguments:
- video_queries: bfloat16 [65536, 1536], P(('grp', 'seq')), may hold values from -18 to 18
- audio_keys: bfloat16 [8192, 1536], P(('grp', 'seq')), may hold values from -10 to 10
- audio_values: bfloat16 [8192, 1536], P(('grp', 'seq')), may hold values from -6 to 6
- grad_video: bfloat16 [65536, 1536], P(('grp', 'seq')), may hold values from -6 to 6
- audio_lists: int32 [512, 8], P(('grp', 'seq')), may hold values from -1 to 255, as said below
Outputs:
- grad_queries: bfloat16 [65536, 1536], P(('grp', 'seq'))
- grad_keys: bfloat16 [8192, 1536], P(('grp', 'seq'))
- grad_values: bfloat16 [8192, 1536], P(('grp', 'seq'))
The draws below stay inside these ranges and needn't reach their ends.
Inputs may be any that keep to these rules, and one draw needn't show every extreme that they name: Each row of audio_lists names 2 to 8 audio blocks that are consecutive numbers in increasing order, followed by -1 entries. Every block named for a video block of device d lies within d - 16 to d + 16.
All inputs are finite; a program needn't handle non-finite values.
Results may differ from the reference program's by a relative error of at most 0.02.
Values may be sent and summed in bfloat16 or wider, within the bound.
A program may use at most 128 MiB of HBM per device.

```python
import jax
import jax.numpy as jnp
from jax import lax

HEADS = 12
HDIM = 128
VBLK = 128
VB_DEV = 2
AUD_DEV = 32
LMAX = 8
RADIUS = 16
VTOK = 65536
NVB = 512
NAUD = 8192
DEVICES = 256


def draw_video_queries(key, part):
    key = jax.random.fold_in(key, 11)
    key_drawn = jax.random.fold_in(key, 0)
    array_shape = (VTOK, HEADS * HDIM)
    result = jnp.clip(jax.random.normal(key_drawn, array_shape, jnp.float32), -6.0, 6.0)
    return result.astype(jnp.bfloat16)


def draw_audio_keys(key, part):
    key = jax.random.fold_in(key, 13)
    key_drawn = jax.random.fold_in(key, 0)
    array_shape = (NAUD, HEADS * HDIM)
    result = jnp.clip(jax.random.normal(key_drawn, array_shape, jnp.float32), -6.0, 6.0)
    return result.astype(jnp.bfloat16)


def draw_audio_lists(key, part):
    key = jax.random.fold_in(key, 5)
    key_length, key_start = jax.random.split(key)
    block_index = jnp.arange(NVB, dtype=jnp.int32)
    owner_device = block_index // VB_DEV
    inner_index = block_index % VB_DEV
    lowest = jnp.maximum(owner_device - RADIUS, 0)
    highest = jnp.minimum(owner_device + RADIUS, DEVICES - 1)
    available = highest - lowest + 1
    length = jnp.minimum(jax.random.randint(key_length, (NVB,), 2, LMAX + 1), available)
    length = jnp.where(block_index == 0, 2, length)
    start_draw = jax.random.randint(key_start, (NVB,), 0, 1 << 20)
    first_block = lowest + start_draw % (available - length + 1)
    from_lowest = (inner_index == 0) & (owner_device % 2 == 0)
    to_highest = (inner_index == VB_DEV - 1) & (owner_device % 2 == 1)
    first_block = jnp.where(from_lowest, lowest, first_block)
    first_block = jnp.where(to_highest, highest - length + 1, first_block)
    first_block = jnp.where(block_index == NVB - 1, highest - length + 1, first_block)
    slot_index = jnp.arange(LMAX, dtype=jnp.int32)[None, :]
    return jnp.where(slot_index < length[:, None], first_block[:, None] + slot_index, -1).astype(jnp.int32)


def block_levels(stream_key, dims, pieces, smallest, high):
    gain = 1.0
    for axis_at, parts in pieces:
        heights = jax.random.uniform(jax.random.fold_in(jax.random.fold_in(stream_key, 6), axis_at), (parts,), jnp.float32, smallest / len(pieces), high / len(pieces))
        gain = gain * jnp.repeat(jnp.exp(heights), dims[axis_at] // parts).reshape((-1,) + (1,) * (len(dims) - 1 - axis_at))
    return gain


def bell_draw(rng, dims, spread, reach, pieces=(), kind=jnp.bfloat16):
    level = block_levels(rng, dims, pieces, -0.22, 0.18) if pieces else 1.0
    drawn = jax.random.normal(rng, dims, jnp.float32) * spread * level
    return jnp.minimum(jnp.maximum(drawn, -reach), reach).astype(kind)


def setup_inputs(seed: int = 0) -> dict:
    arg_keys = jax.random.split(jax.random.key(seed), 6)
    video_queries = draw_video_queries(jax.random.fold_in(arg_keys[5], 71), 0)
    audio_keys = draw_audio_keys(jax.random.fold_in(arg_keys[5], 71), 0)
    audio_values = bell_draw(arg_keys[2], (NAUD, HEADS * HDIM), 1.0, 6.0, ((0, 256),))
    grad_video = bell_draw(arg_keys[3], (VTOK, HEADS * HDIM), 1.0, 6.0, ((0, 256),))
    audio_lists = draw_audio_lists(jax.random.fold_in(arg_keys[5], 71), 0)
    return dict(video_queries=video_queries, audio_keys=audio_keys, audio_values=audio_values, grad_video=grad_video, audio_lists=audio_lists)


MASKED = -1e30


def block_grads(queries, grad_out, key_rows, value_rows, live_keys, head_count):
    blocks, row_count, model_width = queries.shape
    keycount = key_rows.shape[1]
    head_dim = model_width // head_count
    scaling = head_dim ** -0.5
    query_heads = queries.reshape(blocks, row_count, head_count, head_dim).astype(jnp.float32)
    grad_heads = grad_out.reshape(blocks, row_count, head_count, head_dim).astype(jnp.float32)
    key_heads = key_rows.reshape(blocks, keycount, head_count, head_dim).astype(jnp.float32)
    value_heads = value_rows.reshape(blocks, keycount, head_count, head_dim).astype(jnp.float32)
    scores = jnp.einsum("brhd,bkhd->bhrk", query_heads, key_heads) * scaling
    scores = jnp.where(live_keys[:, None, None, :], scores, MASKED)
    row_max = jnp.max(scores, axis=-1, keepdims=True)
    weights = jnp.exp(scores - row_max)
    weights = weights / jnp.sum(weights, axis=-1, keepdims=True)
    weights_low = weights.astype(jnp.bfloat16).astype(jnp.float32)
    value_terms = jnp.einsum("bhrk,brhd->bkhd", weights_low, grad_heads)
    grad_weights = jnp.einsum("brhd,bkhd->bhrk", grad_heads, value_heads)
    row_inner = jnp.sum(weights * grad_weights, axis=-1, keepdims=True)
    grad_scores = (weights * (grad_weights - row_inner) * scaling).astype(jnp.bfloat16).astype(jnp.float32)
    grad_queries = jnp.einsum("bhrk,bkhd->brhd", grad_scores, key_heads)
    key_terms = jnp.einsum("bhrk,brhd->bkhd", grad_scores, query_heads)
    return (grad_queries.reshape(blocks, row_count, model_width),
            key_terms.reshape(blocks, keycount, model_width),
            value_terms.reshape(blocks, keycount, model_width))


def reference(video_queries, audio_keys, audio_values, grad_video, audio_lists):
    model_width = HEADS * HDIM
    padded_keys = jnp.pad(audio_keys.reshape(DEVICES, AUD_DEV, model_width), ((RADIUS, RADIUS), (0, 0), (0, 0)))
    padded_values = jnp.pad(audio_values.reshape(DEVICES, AUD_DEV, model_width), ((RADIUS, RADIUS), (0, 0), (0, 0)))
    query_tiles = video_queries.reshape(DEVICES, VB_DEV, VBLK, model_width)
    grad_tiles = grad_video.reshape(DEVICES, VB_DEV, VBLK, model_width)
    list_tiles = audio_lists.reshape(DEVICES, VB_DEV, LMAX)
    span = 2 * RADIUS + 1

    def one_device(accumulated, inputs):
        device, queries, grad_rows, list_rows = inputs
        valid_slots = list_rows >= 0
        fetch_index = jnp.where(valid_slots, list_rows + RADIUS, 0).astype(jnp.int32).reshape(-1)
        picked_keys = padded_keys[fetch_index].reshape(VB_DEV, LMAX * AUD_DEV, model_width)
        picked_values = padded_values[fetch_index].reshape(VB_DEV, LMAX * AUD_DEV, model_width)
        live_keys = jnp.repeat(valid_slots, AUD_DEV, axis=1)
        grad_queries, key_terms, value_terms = block_grads(queries, grad_rows, picked_keys, picked_values, live_keys, HEADS)
        local_index = jnp.where(valid_slots, list_rows - device + RADIUS, 0).astype(jnp.int32).reshape(-1)
        contrib = jnp.stack([key_terms, value_terms]).reshape(2, VB_DEV * LMAX, AUD_DEV, model_width)
        window = jnp.zeros((2, span, AUD_DEV, model_width), jnp.float32).at[:, local_index].add(contrib)
        rounded = lax.optimization_barrier(window.astype(jnp.bfloat16)).astype(jnp.float32)
        current = lax.dynamic_slice_in_dim(accumulated, device, span, axis=1)
        accumulated = lax.dynamic_update_slice_in_dim(accumulated, current + rounded, device, axis=1)
        return accumulated, grad_queries.astype(jnp.bfloat16)

    initial = jnp.zeros((2, DEVICES + 2 * RADIUS, AUD_DEV, model_width), jnp.float32)
    device_ids = jnp.arange(DEVICES, dtype=jnp.int32)
    accumulated, grad_queries = lax.scan(one_device, initial, (device_ids, query_tiles, grad_tiles, list_tiles))
    sums = accumulated[:, RADIUS:RADIUS + DEVICES].reshape(2, NAUD, model_width)
    return (grad_queries.reshape(VTOK, model_width),
            sums[0].astype(jnp.bfloat16),
            sums[1].astype(jnp.bfloat16))
```

```python
import functools

import jax
import jax.numpy as jnp
from jax import lax
from jax.experimental import pallas as pl
from jax.experimental.pallas import tpu as pltpu
from jax.sharding import PartitionSpec as P

MESH = pl.DeviceIdType.MESH
HEADS = 12
HDIM = 128
NX, NZ, NC = 4, 8, 8
HPD = HEADS // NX
COLS = HPD * HDIM
ROWS = 32
VROWS = 256
VBLK = 128
KEYS = 256
WIN = 2 * NX * NZ
MASKED = -1e30


def position():
    c, s = lax.axis_index("grp"), lax.axis_index("seq")
    return c, s // NZ, s % NZ


def dev(c, x, z):
    return {"grp": c, "seq": x * NZ + z}


def enter(c, x, z):
    barrier = pltpu.get_barrier_semaphore()

    def greet(*where):
        pl.semaphore_signal(barrier, inc=1, device_id=dev(*where), device_id_type=MESH)

    for r in range(1, NX):
        greet(c, (x + r) % NX, z)
    greet(c, x, (z + 1) % NZ)
    greet(c, x, (z + NZ - 1) % NZ)

    @pl.when(c > 0)
    def _():
        greet(c - 1, x, z)

    @pl.when(c < NC - 1)
    def _():
        greet(c + 1, x, z)

    inner = jnp.logical_and(c > 0, c < NC - 1)
    pl.semaphore_wait(barrier, NX - 1 + 2 + 1 + inner.astype(jnp.int32))


def remote(src, dst, sems, at, where):
    return pltpu.make_async_remote_copy(
        src_ref=src,
        dst_ref=dst,
        send_sem=sems[0].at[at],
        recv_sem=sems[1].at[at],
        device_id=dev(*where),
        device_id_type=MESH,
    )


def cols_of(x):
    return pl.ds(pl.multiple_of(x * COLS, COLS), COLS)


def gather_kernel(
    q, g, k, v, info, qg, kv, infos,
    x_send, x_recv, i_send, i_recv, v_send, v_recv, r_send, r_recv, e_send, e_recv, own,
):
    c, x, z = position()
    enter(c, x, z)
    audio, video = (k, v), (q, g)

    started = []

    def go(copy):
        copy.start()
        started.append(copy)
        return copy

    locals_ = []
    for w in range(2):
        copy = pltpu.make_async_copy(audio[w].at[:, cols_of(x)], kv.at[w, 2 + x, z], own.at[w])
        copy.start()
        locals_.append(copy)
    for w in range(2):
        for r in range(1, NX):
            to = (x + r) % NX
            go(remote(audio[w].at[:, cols_of(to)], kv.at[w, 2 + x, z], (x_send, x_recv), (w, r - 1), (c, to, z)))
    for r in range(1, NX):
        go(remote(info, infos.at[x], (i_send, i_recv), r - 1, (c, (x + r) % NX, z)))
    for w in range(2):
        for r in range(1, NX):
            to = (x + r) % NX
            go(remote(video[w].at[:, cols_of(to)], qg.at[w, x], (v_send, v_recv), (w, r - 1), (c, to, z)))
    late = [pltpu.make_async_copy(info, infos.at[x], own.at[4])]
    for w in range(2):
        late.append(pltpu.make_async_copy(video[w].at[:, cols_of(x)], qg.at[w, x], own.at[2 + w]))
    for copy in late:
        copy.start()

    def spread(w, rel):
        zz = (z + rel) % NZ
        up = remote(kv.at[w, pl.ds(4, 2), zz], kv.at[w, pl.ds(0, 2), zz], (e_send, e_recv), (w, 0, rel), (jnp.minimum(c + 1, NC - 1), x, z))
        down = remote(kv.at[w, pl.ds(2, 2), zz], kv.at[w, pl.ds(6, 2), zz], (e_send, e_recv), (w, 1, rel), (jnp.maximum(c - 1, 0), x, z))
        return up, down

    def ring(w, d, step):
        sign = 1 - 2 * d
        panel = kv.at[w, pl.ds(2, NX), (z - sign * step + NZ) % NZ]
        return remote(panel, panel, (r_send, r_recv), (w, d, step), (c, x, (z + sign + NZ) % NZ))

    def arrived(w, d, step):
        sign = 1 - 2 * d
        panel = kv.at[w, pl.ds(2, NX), (z - sign * (step + 1) + 2 * NZ) % NZ]
        remote(panel, panel, (r_send, r_recv), (w, d, step), (c, x, (z + sign + NZ) % NZ)).wait_recv()

    def spread_start(w, rel):
        up, down = spread(w, rel)

        @pl.when(c < NC - 1)
        def _():
            up.start()

        @pl.when(c > 0)
        def _():
            down.start()

    for w in range(2):
        locals_[w].wait()
        for r in range(1, NX):
            came = (x - r + NX) % NX
            remote(audio[w].at[:, cols_of(x)], kv.at[w, 2 + came, z], (x_send, x_recv), (w, r - 1), (c, came, z)).wait_recv()
        for d in range(2):
            go(ring(w, d, 0))
        spread_start(w, 0)
    for step in range(1, 5):
        for w in range(2):
            for d in range(2):
                if step == 4 and w != d:
                    continue
                arrived(w, d, step - 1)
                if step < 3 or (step == 3 and w == d):
                    go(ring(w, d, step))
                spread_start(w, (-step if d == 0 else step) % NZ)

    for copy in late:
        copy.wait()
    for r in range(1, NX):
        came = (x - r + NX) % NX
        remote(info, infos.at[came], (i_send, i_recv), r - 1, (c, came, z)).wait_recv()
        for w in range(2):
            remote(video[w].at[:, cols_of(x)], qg.at[w, came], (v_send, v_recv), (w, r - 1), (c, came, z)).wait_recv()
    for w in range(2):
        for rel in range(NZ):
            up, down = spread(w, rel)

            @pl.when(c < NC - 1)
            def _():
                up.wait_send()
                remote(kv.at[w, pl.ds(6, 2), (z + rel) % NZ], kv.at[w, pl.ds(6, 2), (z + rel) % NZ], (e_send, e_recv), (w, 1, rel), (jnp.minimum(c + 1, NC - 1), x, z)).wait_recv()

            @pl.when(c > 0)
            def _():
                down.wait_send()
                remote(kv.at[w, pl.ds(0, 2), (z + rel) % NZ], kv.at[w, pl.ds(0, 2), (z + rel) % NZ], (e_send, e_recv), (w, 0, rel), (jnp.maximum(c - 1, 0), x, z)).wait_recv()
    for copy in started:
        copy.wait_send()


def nt(a, b):
    return lax.dot_general(a, b, (((1,), (1,)), ((), ())), preferred_element_type=jnp.float32)


def tn(a, b):
    return lax.dot_general(a, b, (((0,), (0,)), ((), ())), preferred_element_type=jnp.float32)


def nn(a, b):
    return lax.dot_general(a, b, (((1,), (0,)), ((), ())), preferred_element_type=jnp.float32)


def compute_kernel(info, qg, kv, dq, out, acc):
    scale = HDIM**-0.5
    acc[...] = jnp.zeros_like(acc)
    key_at = lax.broadcasted_iota(jnp.int32, (KEYS, VBLK), 0)

    def tile(t, _):
        row = (t // 2) * 8 + t % 2
        first = pl.multiple_of(info[row, 0] * ROWS, ROWS)
        live = jnp.logical_and(key_at >= info[row, 1] * ROWS, key_at < info[row, 2] * ROWS)
        rows = pl.ds(pl.multiple_of(t * VBLK, VBLK), VBLK)
        keys = pl.ds(first, KEYS)
        for h in range(HPD):
            cols = pl.ds(h * HDIM, HDIM)
            qt, gt = qg[0, rows, cols], qg[1, rows, cols]
            kt, vt = kv[0, keys, cols], kv[1, keys, cols]
            scores = jnp.where(live, nt(kt, qt) * scale, MASKED)
            raw = jnp.exp(scores - jnp.max(scores, axis=0, keepdims=True))
            weights = raw * (1.0 / jnp.sum(raw, axis=0, keepdims=True))
            grad_weights = nt(vt, gt)
            inner = jnp.sum(weights * grad_weights, axis=0, keepdims=True)
            grad_scores = (weights * (grad_weights - inner) * scale).astype(jnp.bfloat16)
            acc[1, keys, cols] += nn(weights.astype(jnp.bfloat16), gt)
            acc[0, keys, cols] += nn(grad_scores, qt)
            dq[rows, cols] = tn(grad_scores, kt).astype(jnp.bfloat16)
        return 0

    lax.fori_loop(0, 2 * NX, tile, 0)
    out[...] = acc[...].astype(jnp.bfloat16)


def reduce_kernel(
    dq, part, out_q, out_k, out_v,
    edge, moving, landed, final,
    q_send, q_recv, e_send, e_recv, r_send, r_recv, f_send, f_recv, own,
):
    c, x, z = position()
    enter(c, x, z)
    outs = (out_k, out_v)
    started = []

    def go(copy):
        copy.start()
        started.append(copy)
        return copy

    def edges(w, rel):
        zz = (z + rel) % NZ
        up = remote(part.at[w, pl.ds(6, 2), zz], edge.at[w, 0, rel], (e_send, e_recv), (w, 0, rel), (jnp.minimum(c + 1, NC - 1), x, z))
        down = remote(part.at[w, pl.ds(0, 2), zz], edge.at[w, 1, rel], (e_send, e_recv), (w, 1, rel), (jnp.maximum(c - 1, 0), x, z))
        return up, down

    order = (4, 3, 5, 2, 6, 1, 7, 0)
    for rel in order:
        for w in range(2):
            up, down = edges(w, rel)

            @pl.when(c < NC - 1)
            def _():
                up.start()

            @pl.when(c > 0)
            def _():
                down.start()

    @pl.when(c == 0)
    def _():
        edge[:, 0] = jnp.zeros((2,) + edge.shape[2:], edge.dtype)

    @pl.when(c == NC - 1)
    def _():
        edge[:, 1] = jnp.zeros((2,) + edge.shape[2:], edge.dtype)

    for r in range(1, NX):
        to = (x + r) % NX
        go(remote(dq.at[to], out_q.at[:, cols_of(x)], (q_send, q_recv), r - 1, (c, to, z)))
    own_q = pltpu.make_async_copy(dq.at[x], out_q.at[:, cols_of(x)], own.at[2])
    own_q.start()

    def total(w, rel):
        @pl.when(c < NC - 1)
        def _():
            edges(w, rel)[1].wait_recv()

        @pl.when(c > 0)
        def _():
            edges(w, rel)[0].wait_recv()

        mine = part[w, pl.ds(2, NX), (z + rel) % NZ].astype(jnp.float32)
        low = edge[w, 0, rel].astype(jnp.float32)
        high = edge[w, 1, rel].astype(jnp.float32)
        return mine + jnp.concatenate([low, high], axis=0)

    def ring(w, d, dist):
        sign = 1 - 2 * d
        at = (w, d, dist - 1)
        return remote(moving.at[at], landed.at[at], (r_send, r_recv), at, (c, x, (z + sign + NZ) % NZ))

    for dist in range(4, 0, -1):
        for w in range(2):
            for d in range(2):
                if dist == 4 and w != d:
                    continue
                value = total(w, (dist if d == 0 else -dist) % NZ)
                if dist < 3 or (dist == 3 and w == d):
                    ring(w, d, dist + 1).wait_recv()
                    value = value + landed[w, d, dist].astype(jnp.float32)
                moving[w, d, dist - 1] = value.astype(jnp.bfloat16)
                go(ring(w, d, dist))

    def last(w, to, at):
        return remote(final.at[w, to], outs[w].at[:, cols_of(x)], (f_send, f_recv), (w, at), (c, to, z))

    kept = []
    for w in range(2):
        value = total(w, 0)
        for d in range(2):
            ring(w, d, 1).wait_recv()
            value = value + landed[w, d, 0].astype(jnp.float32)
        final[w] = value.astype(jnp.bfloat16)
        for r in range(1, NX):
            go(last(w, (x + r) % NX, r - 1))
        copy = pltpu.make_async_copy(final.at[w, x], outs[w].at[:, cols_of(x)], own.at[w])
        copy.start()
        kept.append(copy)

    own_q.wait()
    for r in range(1, NX):
        came = (x - r + NX) % NX
        remote(dq.at[0], out_q.at[:, cols_of(came)], (q_send, q_recv), r - 1, (c, came, z)).wait_recv()
        for w in range(2):
            remote(final.at[w, 0], outs[w].at[:, cols_of(came)], (f_send, f_recv), (w, r - 1), (c, came, z)).wait_recv()
    for copy in kept:
        copy.wait()
    for w in range(2):
        for rel in range(NZ):
            up, down = edges(w, rel)

            @pl.when(c < NC - 1)
            def _():
                up.wait_send()

            @pl.when(c > 0)
            def _():
                down.wait_send()
    for copy in started:
        copy.wait_send()


ANY = pl.BlockSpec(memory_space=pl.ANY)
VMEM = pl.BlockSpec(memory_space=pltpu.VMEM)
SMEM = pl.BlockSpec(memory_space=pltpu.SMEM)


def sems(*shape):
    return [pltpu.SemaphoreType.DMA(shape)] * 2


def shaped(shape, dtype=jnp.bfloat16):
    return jax.ShapeDtypeStruct(shape, dtype)


def per_device(q, k, v, g, lists):
    c = lax.axis_index("grp")
    first = lists[:, 0] - (c * NX * NZ - WIN // 4)
    count = jnp.sum((lists >= 0).astype(jnp.int32), axis=1)
    highest = jnp.where(c == NC - 1, WIN * 3 // 4, WIN) - 8
    base = jnp.minimum(first, highest)
    info = jnp.stack([base, first - base, first - base + count], axis=1)
    info = jnp.pad(info, ((0, 6), (0, 125)))

    qg, kv, infos = pl.pallas_call(
        gather_kernel,
        out_shape=(
            shaped((2, NX, VROWS, COLS)),
            shaped((2, 8, NZ, ROWS, COLS)),
            shaped((NX, 8, 128), jnp.int32),
        ),
        in_specs=[ANY] * 5,
        out_specs=(ANY,) * 3,
        scratch_shapes=[
            *sems(2, NX - 1), *sems(NX - 1), *sems(2, NX - 1), *sems(2, 2, 4), *sems(2, 2, NZ),
            pltpu.SemaphoreType.DMA((5,)),
        ],
        compiler_params=pltpu.CompilerParams(collective_id=0, has_side_effects=True),
        name="gather",
    )(q, g, k, v, info)

    dq, part = pl.pallas_call(
        compute_kernel,
        out_shape=(shaped((NX * VROWS, COLS)), shaped((2, WIN * ROWS, COLS))),
        in_specs=[SMEM, VMEM, VMEM],
        out_specs=(VMEM, VMEM),
        scratch_shapes=[pltpu.VMEM((2, WIN * ROWS, COLS), jnp.float32)],
        compiler_params=pltpu.CompilerParams(vmem_limit_bytes=40 * 2**20),
        name="compute",
    )(
        infos.reshape(NX * 8, 128),
        qg.reshape(2, NX * VROWS, COLS),
        kv.reshape(2, WIN * ROWS, COLS),
    )

    return pl.pallas_call(
        reduce_kernel,
        out_shape=(shaped(q.shape), shaped(k.shape), shaped(v.shape)),
        in_specs=[ANY, VMEM],
        out_specs=(ANY,) * 3,
        scratch_shapes=[
            pltpu.VMEM((2, 2, NZ, 2, ROWS, COLS), jnp.bfloat16),
            pltpu.VMEM((2, 2, 4, NX, ROWS, COLS), jnp.bfloat16),
            pltpu.VMEM((2, 2, 4, NX, ROWS, COLS), jnp.bfloat16),
            pltpu.VMEM((2, NX, ROWS, COLS), jnp.bfloat16),
            *sems(NX - 1), *sems(2, 2, NZ), *sems(2, 2, 4), *sems(2, NX - 1),
            pltpu.SemaphoreType.DMA((3,)),
        ],
        compiler_params=pltpu.CompilerParams(
            collective_id=1, has_side_effects=True, vmem_limit_bytes=40 * 2**20
        ),
        name="reduce",
    )(dq.reshape(NX, VROWS, COLS), part.reshape(2, 8, NZ, ROWS, COLS))


def solution(mesh):
    placed = P(("grp", "seq"), None)
    return jax.shard_map(
        per_device,
        mesh=mesh,
        in_specs=(placed,) * 5,
        out_specs=(placed,) * 3,
        check_vma=False,
    )
```

```python
import jax
import jax.numpy as jnp
from jax import lax
from jax.experimental import pallas as pl
from jax.experimental.pallas import tpu as pltpu
from jax.sharding import PartitionSpec as P

MESH = pl.DeviceIdType.MESH
HEADS = 12
HDIM = 128
NX, NZ, NC = 4, 8, 8
HPD = HEADS // NX
ROWS = 32
VROWS = 256
VBLK = 128
LMAX = 8
KEYS = LMAX * ROWS
WIN = 2 * NX * NZ
TILES = 2 * NX
MASKED = -1e30
BF16 = jnp.bfloat16


def dev(c, x, z):
    return {"grp": c, "seq": x * NZ + z}


def enter(c, x, z):
    barrier = pltpu.get_barrier_semaphore()

    def greet(*where):
        pl.semaphore_signal(barrier, inc=1, device_id=dev(*where), device_id_type=MESH)

    for r in range(1, NX):
        greet(c, (x + r) % NX, z)
    greet(c, x, (z + 1) % NZ)
    greet(c, x, (z + NZ - 1) % NZ)

    @pl.when(c > 0)
    def _():
        greet(c - 1, x, z)

    @pl.when(c < NC - 1)
    def _():
        greet(c + 1, x, z)

    inner = jnp.logical_and(c > 0, c < NC - 1)
    pl.semaphore_wait(barrier, NX - 1 + 2 + 1 + inner.astype(jnp.int32))


def remote(src, dst, sems, at, where):
    return pltpu.make_async_remote_copy(
        src_ref=src,
        dst_ref=dst,
        send_sem=sems[0].at[at],
        recv_sem=sems[1].at[at],
        device_id=dev(*where),
        device_id_type=MESH,
    )


def head_cols(x, h):
    return pl.ds(pl.multiple_of((x * HPD + h) * HDIM, HDIM), HDIM)


def nt(a, b):
    return lax.dot_general(a, b, (((1,), (1,)), ((), ())), preferred_element_type=jnp.float32)


def tn(a, b):
    return lax.dot_general(a, b, (((0,), (0,)), ((), ())), preferred_element_type=jnp.float32)


def nn(a, b):
    return lax.dot_general(a, b, (((1,), (0,)), ((), ())), preferred_element_type=jnp.float32)


def kernel(
    q, g, k, v, lists, out_q, out_k, out_v,
    kv0, kv1, kv2, qg0, qg1, qg2, dq0, dq1, dq2, part0, part1, part2, edge0, edge1, edge2,
    moving0, moving1, moving2, landed0, landed1, landed2, final0, final1, final2,
    pads, mine, lists_v, lists_s, runs,
    k_send, k_recv, i_send, i_recv, v_send, v_recv, r_send, r_recv, e_send, e_recv,
    q_send, q_recv, b_send, b_recv, s_send, s_recv, f_send, f_recv, own_k, own_v, own_q, own_f, own_i,
):
    c, s = lax.axis_index("grp"), lax.axis_index("seq")
    x, z = s // NZ, s % NZ
    enter(c, x, z)
    audio, video, outs = (k, v), (q, g), (out_k, out_v)
    kv, qg, dq = (kv0, kv1, kv2), (qg0, qg1, qg2), (dq0, dq1, dq2)
    part, edge = (part0, part1, part2), (edge0, edge1, edge2)
    moving, landed, final = (moving0, moving1, moving2), (landed0, landed1, landed2), (final0, final1, final2)
    above, below = jnp.minimum(c + 1, NC - 1), jnp.maximum(c - 1, 0)
    has_above, has_below = c < NC - 1, c > 0
    started, kept = [], []

    def go(copy):
        copy.start()
        started.append(copy)

    def peers():
        return [(r - 1, (x + r) % NX, (x - r + NX) % NX) for r in range(1, NX)]

    def audio_copy(h, w, r, to, came):
        return remote(audio[w].at[:, head_cols(to, h)], kv[h].at[w, 2 + came, z], (k_send, k_recv), (h, w, r), (c, to, z))

    def video_copy(h, w, r, to, came):
        return remote(video[w].at[:, head_cols(to, h)], qg[h].at[w, came], (v_send, v_recv), (h, w, r), (c, to, z))

    def own_audio(h, w):
        return pltpu.make_async_copy(audio[w].at[:, head_cols(x, h)], kv[h].at[w, 2 + x, z], own_k.at[h, w])

    def own_video(h, w):
        return pltpu.make_async_copy(video[w].at[:, head_cols(x, h)], qg[h].at[w, x], own_v.at[h, w])

    def list_copy(r, to, came):
        return remote(mine, lists_v.at[came], (i_send, i_recv), r, (c, to, z))

    def ring(h, w, d, step, at):
        panel = kv[h].at[w, pl.ds(2, NX), (z + at) % NZ]
        return remote(panel, panel, (r_send, r_recv), (h, w, d, step), (c, x, (z + 1 - 2 * d + NZ) % NZ))

    def spread(h, w, rel):
        zz = (z + rel) % NZ

        @pl.when(has_above)
        def _():
            remote(kv[h].at[w, pl.ds(4, 2), zz], kv[h].at[w, pl.ds(0, 2), zz], (e_send, e_recv), (h, w, 0), (above, x, z)).start()

        @pl.when(has_below)
        def _():
            remote(kv[h].at[w, pl.ds(2, 2), zz], kv[h].at[w, pl.ds(6, 2), zz], (e_send, e_recv), (h, w, 1), (below, x, z)).start()

    def spread_wait(h, w, sent):
        @pl.when(has_above)
        def _():
            up = remote(kv[h].at[w, pl.ds(4, 2)], kv[h].at[w, pl.ds(0, 2)], (e_send, e_recv), (h, w, 0), (above, x, z))
            down = remote(kv[h].at[w, pl.ds(2, 2)], kv[h].at[w, pl.ds(6, 2)], (e_send, e_recv), (h, w, 1), (above, x, z))
            up.wait_send() if sent else down.wait_recv()

        @pl.when(has_below)
        def _():
            up = remote(kv[h].at[w, pl.ds(4, 2)], kv[h].at[w, pl.ds(0, 2)], (e_send, e_recv), (h, w, 0), (below, x, z))
            down = remote(kv[h].at[w, pl.ds(2, 2)], kv[h].at[w, pl.ds(6, 2)], (e_send, e_recv), (h, w, 1), (below, x, z))
            down.wait_send() if sent else up.wait_recv()

    for h in range(HPD):
        for w in range(2):
            for peer in peers():
                go(audio_copy(h, w, *peer[:2], x))
            own_audio(h, w).start()
    mine[...] = jnp.zeros_like(mine)
    mine[0:2, 0:LMAX] = lists[...]
    for peer in peers():
        go(list_copy(*peer[:2], x))
    pltpu.make_async_copy(mine, lists_v.at[x], own_i.at[0]).start()

    for h in range(HPD):
        for w in range(2):
            own_audio(h, w).wait()
            for peer in peers():
                audio_copy(h, w, *peer).wait_recv()
            for d in range(2):
                go(ring(h, w, d, 0, 0))
            spread(h, w, 0)
        if h == 0:
            for w in range(2):
                for peer in peers():
                    go(video_copy(h, w, *peer[:2], x))
                own_video(h, w).start()
    pads[:, :, 0:LMAX] = jnp.zeros((TILES, 2, LMAX, ROWS, HDIM), jnp.float32)
    pads[:, :, 2 * LMAX : 3 * LMAX] = jnp.zeros((TILES, 2, LMAX, ROWS, HDIM), jnp.float32)
    for h in range(HPD):

        @pl.when(c == 0)
        def _():
            edge[h][:, 0] = jnp.zeros((2,) + edge[h].shape[2:], BF16)

        @pl.when(c == NC - 1)
        def _():
            edge[h][:, 1] = jnp.zeros((2,) + edge[h].shape[2:], BF16)

    for step in range(1, 5):
        for h in range(HPD):
            for w in range(2):
                for d in range(2):
                    if step == 4 and w != d:
                        continue
                    rel = step if d else -step
                    ring(h, w, d, step - 1, rel + NZ).wait_recv()
                    if step < 3 or (step == 3 and w == d):
                        go(ring(h, w, d, step, rel + NZ))
                    spread(h, w, rel + NZ)
        if step < HPD:
            for w in range(2):
                for peer in peers():
                    go(video_copy(step, w, *peer[:2], x))
                own_video(step, w).start()

    pltpu.make_async_copy(mine, lists_v.at[x], own_i.at[0]).wait()
    for peer in peers():
        list_copy(*peer).wait_recv()
    fetched = pltpu.make_async_copy(lists_v, lists_s, own_i.at[1])
    fetched.start()
    fetched.wait()
    for t in range(TILES):
        count = jnp.int32(0)
        for j in range(LMAX):
            count += (lists_s[t // 2, t % 2, j] >= 0).astype(jnp.int32)
        runs[0, t] = jnp.clip(lists_s[t // 2, t % 2, 0] - (c * NX * NZ - NX * NZ // 2), 0, WIN - 1)
        runs[1, t] = count

    scale = HDIM**-0.5
    key_at = lax.broadcasted_iota(jnp.int32, (KEYS, VBLK), 0)

    def tiles(h, low, high):
        def pair(xd, _):
            for b in range(2):
                t = xd * 2 + b
                first, count = runs[0, t], runs[1, t]
                blocks = [jnp.minimum(first + jnp.where(j < count, j, 0), WIN - 1) for j in range(LMAX)]
                kt = jnp.concatenate([kv[h][0, e >> 3, e & 7] for e in blocks], axis=0)
                vt = jnp.concatenate([kv[h][1, e >> 3, e & 7] for e in blocks], axis=0)
                qt, gt = qg[h][0, xd, b * VBLK : (b + 1) * VBLK], qg[h][1, xd, b * VBLK : (b + 1) * VBLK]
                scores = jnp.where(key_at < count * ROWS, nt(kt, qt) * scale, MASKED)
                raw = jnp.exp(scores - jnp.max(scores, axis=0, keepdims=True))
                weights = raw * (1.0 / jnp.sum(raw, axis=0, keepdims=True))
                grad_weights = nt(vt, gt)
                inner = jnp.sum(weights * grad_weights, axis=0, keepdims=True)
                grad_scores = (weights * (grad_weights - inner) * scale).astype(BF16)
                pads[t, 1, LMAX : 2 * LMAX] = nn(weights.astype(BF16), gt).reshape(LMAX, ROWS, HDIM)
                pads[t, 0, LMAX : 2 * LMAX] = nn(grad_scores, qt).reshape(LMAX, ROWS, HDIM)
                dq[h][xd, b * VBLK : (b + 1) * VBLK] = tn(grad_scores, kt).astype(BF16)
            return 0

        lax.fori_loop(low, high, pair, 0)

    def place(h):
        for w in range(2):
            for line in range(2 * NX):
                near = range(max(0, line - NX) * 2, min(NX, line + 1) * 2)
                total = None
                for t in near:
                    term = pads[t, w, pl.ds(jnp.clip(line * NZ - runs[0, t] + LMAX, 0, 2 * LMAX), LMAX)]
                    total = term if total is None else total + term
                part[h][w, line] = total.astype(BF16)

    def query_copy(h, r, to, mine_at):
        return remote(dq[h].at[to], out_q.at[:, head_cols(mine_at, h)], (q_send, q_recv), (h, r), (c, to, z))

    def own_query(h):
        return pltpu.make_async_copy(dq[h].at[x], out_q.at[:, head_cols(x, h)], own_q.at[h])

    def edge_copy(h, w, d):
        line, to = ((6, above), (0, below))[d]
        return remote(part[h].at[w, pl.ds(line, 2)], edge[h].at[w, d], (b_send, b_recv), (h, w, d), (to, x, z))

    def hand_out(h):
        for w in range(2):

            @pl.when(has_above)
            def _():
                edge_copy(h, w, 0).start()

            @pl.when(has_below)
            def _():
                edge_copy(h, w, 1).start()

        for peer in peers():
            go(query_copy(h, *peer[:2], x))
        own_query(h).start()

    def edges_in(h, w):
        @pl.when(has_above)
        def _():
            edge_copy(h, w, 1).wait_recv()

        @pl.when(has_below)
        def _():
            edge_copy(h, w, 0).wait_recv()

    def total(h, w, rel):
        zz = (z + rel + NZ) % NZ
        low = part[h][w, 2:4, zz].astype(jnp.float32) + edge[h][w, 0, :, zz].astype(jnp.float32)
        high = part[h][w, 4:6, zz].astype(jnp.float32) + edge[h][w, 1, :, zz].astype(jnp.float32)
        return jnp.concatenate([low, high], axis=0)

    def sum_ring(h, w, d, dist):
        at = (w, d, dist - 1)
        return remote(moving[h].at[at], landed[h].at[at], (s_send, s_recv), (h, *at), (c, x, (z + 1 - 2 * d + NZ) % NZ))

    def sums(h, dist):
        for w in range(2):
            if dist == 4:
                edges_in(h, w)
            for d in range(2):
                if dist == 4 and w != d:
                    continue
                value = total(h, w, -dist if d else dist)
                if dist < 3 or (dist == 3 and w == d):
                    sum_ring(h, w, d, dist + 1).wait_recv()
                    value = value + landed[h][w, d, dist].astype(jnp.float32)
                moving[h][w, d, dist - 1] = value.astype(BF16)
                go(sum_ring(h, w, d, dist))

    def final_copy(h, w, r, to, mine_at):
        return remote(final[h].at[w, to], outs[w].at[:, head_cols(mine_at, h)], (f_send, f_recv), (h, w, r), (c, to, z))

    def own_final(h, w):
        return pltpu.make_async_copy(final[h].at[w, x], outs[w].at[:, head_cols(x, h)], own_f.at[h, w])

    def finish(h):
        for w in range(2):
            value = total(h, w, 0)
            for d in range(2):
                sum_ring(h, w, d, 1).wait_recv()
                value = value + landed[h][w, d, 0].astype(jnp.float32)
            final[h][w] = value.astype(BF16)
            for peer in peers():
                go(final_copy(h, w, *peer[:2], x))
            own_final(h, w).start()

    def ready(h):
        for w in range(2):
            spread_wait(h, w, False)
            own_video(h, w).wait()
            for peer in peers():
                video_copy(h, w, *peer).wait_recv()

    def compute(h, between):
        ready(h)
        half = NX // 2
        tiles(h, 0, half)
        between[0]()
        tiles(h, half, NX)
        between[1]()
        place(h)
        hand_out(h)

    nothing = lambda: None
    compute(0, (nothing, nothing))
    compute(1, (nothing, lambda: sums(0, 4)))
    compute(2, (lambda: sums(0, 3), lambda: sums(0, 2)))
    sums(1, 4)
    sums(0, 1)
    sums(1, 3)
    sums(2, 4)
    finish(0)
    sums(1, 2)
    sums(2, 3)
    sums(1, 1)
    sums(2, 2)
    finish(1)
    sums(2, 1)
    finish(2)

    for h in range(HPD):
        own_query(h).wait()
        for peer in peers():
            r, to, came = peer
            query_copy(h, r, to, came).wait_recv()
        for w in range(2):
            spread_wait(h, w, True)
            own_final(h, w).wait()
            for r, to, came in peers():
                final_copy(h, w, r, to, came).wait_recv()

            @pl.when(has_above)
            def _():
                edge_copy(h, w, 0).wait_send()

            @pl.when(has_below)
            def _():
                edge_copy(h, w, 1).wait_send()

    for copy in started:
        copy.wait_send()


ANY = pl.BlockSpec(memory_space=pl.ANY)
VMEM = pl.BlockSpec(memory_space=pltpu.VMEM)


def sems(*shape):
    return [pltpu.SemaphoreType.DMA(shape)] * 2


def each(*shape):
    return [pltpu.VMEM(shape, BF16)] * HPD


def per_device(q, k, v, g, lists):
    return pl.pallas_call(
        kernel,
        out_shape=tuple(jax.ShapeDtypeStruct(a.shape, BF16) for a in (q, k, v)),
        in_specs=[ANY] * 4 + [VMEM],
        out_specs=(ANY,) * 3,
        scratch_shapes=[
            *each(2, 2 * NX, NZ, ROWS, HDIM),
            *each(2, NX, VROWS, HDIM),
            *each(NX, VROWS, HDIM),
            *each(2, 2 * NX, NZ, ROWS, HDIM),
            *each(2, 2, 2, NZ, ROWS, HDIM),
            *each(2, 2, 4, NX, ROWS, HDIM),
            *each(2, 2, 4, NX, ROWS, HDIM),
            *each(2, NX, ROWS, HDIM),
            pltpu.VMEM((TILES, 2, 3 * LMAX, ROWS, HDIM), jnp.float32),
            pltpu.VMEM((8, 128), jnp.int32),
            pltpu.VMEM((NX, 8, 128), jnp.int32),
            pltpu.SMEM((NX, 8, 128), jnp.int32),
            pltpu.SMEM((2, TILES), jnp.int32),
            *sems(HPD, 2, NX - 1), *sems(NX - 1), *sems(HPD, 2, NX - 1), *sems(HPD, 2, 2, 4), *sems(HPD, 2, 2),
            *sems(HPD, NX - 1), *sems(HPD, 2, 2), *sems(HPD, 2, 2, 4), *sems(HPD, 2, NX - 1),
            pltpu.SemaphoreType.DMA((HPD, 2)),
            pltpu.SemaphoreType.DMA((HPD, 2)),
            pltpu.SemaphoreType.DMA((HPD,)),
            pltpu.SemaphoreType.DMA((HPD, 2)),
            pltpu.SemaphoreType.DMA((2,)),
        ],
        compiler_params=pltpu.CompilerParams(
            collective_id=0, has_side_effects=True, vmem_limit_bytes=48 * 2**20
        ),
        name="cross_attention_backward",
    )(q, g, k, v, lists)


def solution(mesh):
    placed = P(("grp", "seq"), None)
    return jax.shard_map(
        per_device,
        mesh=mesh,
        in_specs=(placed,) * 5,
        out_specs=(placed,) * 3,
        check_vma=False,
    )
```

```python
import jax
import jax.numpy as jnp
from jax import lax
from jax.experimental import pallas as pl
from jax.experimental.pallas import tpu as pltpu
from jax.sharding import PartitionSpec as P

MESH = pl.DeviceIdType.MESH
HEADS = 12
HDIM = 128
NX, NZ, NC = 4, 8, 8
HPD = HEADS // NX
ROWS = 32
VROWS = 256
VBLK = 128
LMAX = 8
KEYS = LMAX * ROWS
WIN = 2 * NX * NZ
TILES = 2 * NX
SPREADS = ((0, 5), (5, 2), (7, 1))
EDGES = ((5, 3), (0, 5))
MASKED = -1e30
LOG2E = 1.4426950408889634
BF16 = jnp.bfloat16


def dev(c, x, z):
    return {"grp": c, "seq": x * NZ + z}


def enter(c, x, z):
    barrier = pltpu.get_barrier_semaphore()

    def greet(*where):
        pl.semaphore_signal(barrier, inc=1, device_id=dev(*where), device_id_type=MESH)

    for r in range(1, NX):
        greet(c, (x + r) % NX, z)
    greet(c, x, (z + 1) % NZ)
    greet(c, x, (z + NZ - 1) % NZ)

    @pl.when(c > 0)
    def _():
        greet(c - 1, x, z)

    @pl.when(c < NC - 1)
    def _():
        greet(c + 1, x, z)

    inner = jnp.logical_and(c > 0, c < NC - 1)
    pl.semaphore_wait(barrier, NX - 1 + 2 + 1 + inner.astype(jnp.int32))


def remote(src, dst, sems, at, where):
    return pltpu.make_async_remote_copy(
        src_ref=src,
        dst_ref=dst,
        send_sem=sems[0].at[at],
        recv_sem=sems[1].at[at],
        device_id=dev(*where),
        device_id_type=MESH,
    )


def at(rel):
    return NZ - 1 if abs(rel) == 4 else 2 * rel if rel >= 0 else -2 * rel - 1


def head_cols(x, h):
    return pl.ds(pl.multiple_of((x * HPD + h) * HDIM, HDIM), HDIM)


def nt(a, b):
    return lax.dot_general(a, b, (((1,), (1,)), ((), ())), preferred_element_type=jnp.float32)


def tn(a, b):
    return lax.dot_general(a, b, (((0,), (0,)), ((), ())), preferred_element_type=jnp.float32)


def nn(a, b):
    return lax.dot_general(a, b, (((1,), (0,)), ((), ())), preferred_element_type=jnp.float32)


def kernel(
    q, g, k, v, lists, out_q, out_k, out_v,
    kv0, kv1, kv2, qg0, qg1, qg2, dq0, dq1, dq2, part0, part1, part2, edge0, edge1, edge2,
    moving0, moving1, moving2, landed0, landed1, landed2, final0, final1, final2,
    pads, mine, lists_v, lists_s, runs,
    k_send, k_recv, i_send, i_recv, v_send, v_recv, r_send, r_recv, e_send, e_recv,
    q_send, q_recv, b_send, b_recv, s_send, s_recv, f_send, f_recv, own_k, own_v, own_q, own_f, own_i,
):
    c, s = lax.axis_index("grp"), lax.axis_index("seq")
    x, z = s // NZ, s % NZ
    enter(c, x, z)
    audio, video, outs = (k, v), (q, g), (out_k, out_v)
    kv, qg, dq = (kv0, kv1, kv2), (qg0, qg1, qg2), (dq0, dq1, dq2)
    part, edge = (part0, part1, part2), (edge0, edge1, edge2)
    moving, landed, final = (moving0, moving1, moving2), (landed0, landed1, landed2), (final0, final1, final2)
    above, below = jnp.minimum(c + 1, NC - 1), jnp.maximum(c - 1, 0)
    has_above, has_below = c < NC - 1, c > 0
    started, kept = [], []

    def go(copy):
        copy.start()
        started.append(copy)

    def peers():
        return [(r - 1, (x + r) % NX, (x - r + NX) % NX) for r in range(1, NX)]

    def audio_copy(h, w, r, to, came):
        return remote(audio[w].at[:, head_cols(to, h)], kv[h].at[w, 2 + came, 0], (k_send, k_recv), (h, w, r), (c, to, z))

    def video_copy(h, w, r, to, came):
        return remote(video[w].at[:, head_cols(to, h)], qg[h].at[w, came], (v_send, v_recv), (h, w, r), (c, to, z))

    def own_audio(h, w):
        return pltpu.make_async_copy(audio[w].at[:, head_cols(x, h)], kv[h].at[w, 2 + x, 0], own_k.at[h, w])

    def own_video(h, w):
        return pltpu.make_async_copy(video[w].at[:, head_cols(x, h)], qg[h].at[w, x], own_v.at[h, w])

    def list_copy(r, to, came):
        return remote(mine, lists_v.at[came], (i_send, i_recv), r, (c, to, z))

    def ring(h, w, d, step):
        sign = 1 - 2 * d
        source = kv[h].at[w, pl.ds(2, NX), at(-sign * step)]
        target = kv[h].at[w, pl.ds(2, NX), at(-sign * (step + 1))]
        return remote(source, target, (r_send, r_recv), (h, w, d, step), (c, x, (z + sign + NZ) % NZ))

    def spread_copy(h, w, d, part_of):
        low, count = SPREADS[part_of]
        span = pl.ds(low, count)
        line, there, to = ((4, 0, above), (2, 6, below))[d]
        source, target = kv[h].at[w, pl.ds(line, 2), span], kv[h].at[w, pl.ds(there, 2), span]
        return remote(source, target, (e_send, e_recv), (h, w, d, part_of), (to, x, z))

    def spread(h, w, part_of):
        @pl.when(has_above)
        def _():
            spread_copy(h, w, 0, part_of).start()

        @pl.when(has_below)
        def _():
            spread_copy(h, w, 1, part_of).start()

    def spread_wait(h, w, sent):
        for part_of in range(len(SPREADS)):

            @pl.when(has_above)
            def _():
                spread_copy(h, w, 0, part_of).wait_send() if sent else spread_copy(h, w, 1, part_of).wait_recv()

            @pl.when(has_below)
            def _():
                spread_copy(h, w, 1, part_of).wait_send() if sent else spread_copy(h, w, 0, part_of).wait_recv()

    for h in range(HPD):
        for w in range(2):
            for peer in peers():
                go(audio_copy(h, w, *peer[:2], x))
            own_audio(h, w).start()
    mine[...] = jnp.zeros_like(mine)
    mine[0:2, 0:LMAX] = lists[...]
    for peer in peers():
        go(list_copy(*peer[:2], x))
    pltpu.make_async_copy(mine, lists_v.at[x], own_i.at[0]).start()

    for h in range(HPD):
        for w in range(2):
            own_audio(h, w).wait()
            for peer in peers():
                audio_copy(h, w, *peer).wait_recv()
            for d in range(2):
                go(ring(h, w, d, 0))
        if h == 0:
            for w in range(2):
                for peer in peers():
                    go(video_copy(h, w, *peer[:2], x))
                own_video(h, w).start()
    pads[:, :, 0:LMAX] = jnp.zeros((TILES, 2, LMAX, ROWS, HDIM), jnp.float32)
    pads[:, :, 2 * LMAX : 3 * LMAX] = jnp.zeros((TILES, 2, LMAX, ROWS, HDIM), jnp.float32)
    for h in range(HPD):

        @pl.when(c == 0)
        def _():
            edge[h][:, 0] = jnp.zeros((2,) + edge[h].shape[2:], BF16)

        @pl.when(c == NC - 1)
        def _():
            edge[h][:, 1] = jnp.zeros((2,) + edge[h].shape[2:], BF16)

    for step in range(1, 5):
        for h in range(HPD):
            for w in range(2):
                for d in range(2):
                    if step == 4 and w != d:
                        continue
                    ring(h, w, d, step - 1).wait_recv()
                    if step < 3 or (step == 3 and w == d):
                        go(ring(h, w, d, step))
                if step > 1:
                    spread(h, w, step - 2)
        if step < HPD:
            for w in range(2):
                for peer in peers():
                    go(video_copy(step, w, *peer[:2], x))
                own_video(step, w).start()

    pltpu.make_async_copy(mine, lists_v.at[x], own_i.at[0]).wait()
    for peer in peers():
        list_copy(*peer).wait_recv()
    fetched = pltpu.make_async_copy(lists_v, lists_s, own_i.at[1])
    fetched.start()
    fetched.wait()
    for t in range(TILES):
        count = jnp.int32(0)
        for j in range(LMAX):
            count += (lists_s[t // 2, t % 2, j] >= 0).astype(jnp.int32)
        runs[0, t] = jnp.clip(lists_s[t // 2, t % 2, 0] - (c * NX * NZ - NX * NZ // 2), 0, WIN - 1)
        runs[1, t] = count

    scale = HDIM**-0.5

    def tiles(h):
        loaded, ready_terms = [], []
        for t in range(TILES):
            first, count = runs[0, t], runs[1, t]
            blocks = [jnp.minimum(first + jnp.where(j < count, j, 0), WIN - 1) for j in range(LMAX)]
            places = [(e >> 3, ((e & 7) - z + NZ) & 7) for e in blocks]
            places = [(line, jnp.where(rel < 4, 2 * rel, 15 - 2 * rel)) for line, rel in places]
            kt = jnp.concatenate([kv[h][0, line, where] for line, where in places], axis=0)
            vt = jnp.concatenate([kv[h][1, line, where] for line, where in places], axis=0)
            rows = pl.ds(t % 2 * VBLK, VBLK)
            qt, gt = qg[h][0, t // 2, rows], qg[h][1, t // 2, rows]
            loaded.append((count, kt, qt, gt, nt(kt, qt), nt(vt, gt)))
        for count, kt, qt, gt, products, grad_weights in loaded:
            dead = [jnp.full((ROWS, VBLK), jnp.where(j < count, 0.0, MASKED), jnp.float32) for j in range(LMAX)]
            scores = products * (scale * LOG2E) + jnp.concatenate(dead, axis=0)
            raw = jnp.exp2(scores - jnp.max(scores, axis=0, keepdims=True))
            inverse = 1.0 / jnp.sum(raw, axis=0, keepdims=True)
            inner = jnp.sum(raw * grad_weights, axis=0, keepdims=True) * inverse
            weights_low = (raw * inverse).astype(BF16)
            grad_scores = (raw * ((grad_weights - inner) * (inverse * scale))).astype(BF16)
            ready_terms.append((kt, qt, gt, weights_low, grad_scores))
        for t, (kt, qt, gt, weights_low, grad_scores) in enumerate(ready_terms):
            pads[t, 1, LMAX : 2 * LMAX] = nn(weights_low, gt).reshape(LMAX, ROWS, HDIM)
            pads[t, 0, LMAX : 2 * LMAX] = nn(grad_scores, qt).reshape(LMAX, ROWS, HDIM)
            dq[h][t // 2, pl.ds(t % 2 * VBLK, VBLK)] = tn(grad_scores, kt).astype(BF16)

    def place(h):
        for w in range(2):
            for line in range(2 * NX):
                near = range(max(0, line - NX) * 2, min(NX, line + 1) * 2)
                total = None
                for t in near:
                    term = pads[t, w, pl.ds(jnp.clip(line * NZ - runs[0, t] + LMAX, 0, 2 * LMAX), LMAX)]
                    total = term if total is None else total + term
                total = total.astype(BF16)
                for zz in range(NZ):
                    rel = (zz - z + NZ) & 7
                    part[h][w, line, jnp.where(rel < 4, 2 * rel, 15 - 2 * rel)] = total[zz]

    def query_copy(h, r, to, mine_at):
        return remote(dq[h].at[to], out_q.at[:, head_cols(mine_at, h)], (q_send, q_recv), (h, r), (c, to, z))

    def own_query(h):
        return pltpu.make_async_copy(dq[h].at[x], out_q.at[:, head_cols(x, h)], own_q.at[h])

    def edge_copy(h, w, d, part_of):
        low, count = EDGES[part_of]
        line, to = ((6, above), (0, below))[d]
        source, target = part[h].at[w, pl.ds(line, 2), pl.ds(low, count)], edge[h].at[w, d, :, pl.ds(low, count)]
        return remote(source, target, (b_send, b_recv), (h, w, d, part_of), (to, x, z))

    def hand_out(h):
        for part_of in range(len(EDGES)):
            for w in range(2):

                @pl.when(has_above)
                def _():
                    edge_copy(h, w, 0, part_of).start()

                @pl.when(has_below)
                def _():
                    edge_copy(h, w, 1, part_of).start()

        for peer in peers():
            go(query_copy(h, *peer[:2], x))
        own_query(h).start()

    def edges_in(h, w, part_of):
        @pl.when(has_above)
        def _():
            edge_copy(h, w, 1, part_of).wait_recv()

        @pl.when(has_below)
        def _():
            edge_copy(h, w, 0, part_of).wait_recv()

    def total(h, w, rel):
        p = at(rel)
        low = part[h][w, 2:4, p].astype(jnp.float32) + edge[h][w, 0, :, p].astype(jnp.float32)
        high = part[h][w, 4:6, p].astype(jnp.float32) + edge[h][w, 1, :, p].astype(jnp.float32)
        return jnp.concatenate([low, high], axis=0)

    def sum_ring(h, w, d, dist):
        slot = (w, d, dist - 1)
        return remote(moving[h].at[slot], landed[h].at[slot], (s_send, s_recv), (h, *slot), (c, x, (z + 1 - 2 * d + NZ) % NZ))

    def sums(h, dist):
        for w in range(2):
            if dist in (4, 2):
                edges_in(h, w, 0 if dist == 4 else 1)
            for d in range(2):
                if dist == 4 and w != d:
                    continue
                value = total(h, w, -dist if d else dist)
                if dist < 3 or (dist == 3 and w == d):
                    sum_ring(h, w, d, dist + 1).wait_recv()
                    value = value + landed[h][w, d, dist].astype(jnp.float32)
                moving[h][w, d, dist - 1] = value.astype(BF16)
                go(sum_ring(h, w, d, dist))

    def final_copy(h, w, r, to, mine_at):
        return remote(final[h].at[w, to], outs[w].at[:, head_cols(mine_at, h)], (f_send, f_recv), (h, w, r), (c, to, z))

    def own_final(h, w):
        return pltpu.make_async_copy(final[h].at[w, x], outs[w].at[:, head_cols(x, h)], own_f.at[h, w])

    def finish(h):
        for w in range(2):
            value = total(h, w, 0)
            for d in range(2):
                sum_ring(h, w, d, 1).wait_recv()
                value = value + landed[h][w, d, 0].astype(jnp.float32)
            final[h][w] = value.astype(BF16)
            for peer in peers():
                go(final_copy(h, w, *peer[:2], x))
            own_final(h, w).start()

    def ready(h):
        for w in range(2):
            spread_wait(h, w, False)
            own_video(h, w).wait()
            for peer in peers():
                video_copy(h, w, *peer).wait_recv()

    def compute(h):
        ready(h)
        tiles(h)
        place(h)
        hand_out(h)

    compute(0)
    compute(1)
    sums(0, 4)
    compute(2)
    sums(1, 4)
    sums(2, 4)
    for dist in (3, 2, 1):
        for h in range(HPD):
            sums(h, dist)
    for h in range(HPD):
        finish(h)

    for h in range(HPD):
        own_query(h).wait()
        for peer in peers():
            r, to, came = peer
            query_copy(h, r, to, came).wait_recv()
        for w in range(2):
            spread_wait(h, w, True)
            own_final(h, w).wait()
            for r, to, came in peers():
                final_copy(h, w, r, to, came).wait_recv()

            for part_of in range(len(EDGES)):

                @pl.when(has_above)
                def _():
                    edge_copy(h, w, 0, part_of).wait_send()

                @pl.when(has_below)
                def _():
                    edge_copy(h, w, 1, part_of).wait_send()

    for copy in started:
        copy.wait_send()


HBM = pl.BlockSpec(memory_space=pltpu.HBM)
VMEM = pl.BlockSpec(memory_space=pltpu.VMEM)


def sems(*shape):
    return [pltpu.SemaphoreType.DMA(shape)] * 2


def each(*shape):
    return [pltpu.VMEM(shape, BF16)] * HPD


def per_device(q, k, v, g, lists):
    return pl.pallas_call(
        kernel,
        out_shape=tuple(jax.ShapeDtypeStruct(a.shape, BF16) for a in (q, k, v)),
        in_specs=[HBM] * 4 + [VMEM],
        out_specs=(HBM,) * 3,
        scratch_shapes=[
            *each(2, 2 * NX, NZ, ROWS, HDIM),
            *each(2, NX, VROWS, HDIM),
            *each(NX, VROWS, HDIM),
            *each(2, 2 * NX, NZ, ROWS, HDIM),
            *each(2, 2, 2, NZ, ROWS, HDIM),
            *each(2, 2, 4, NX, ROWS, HDIM),
            *each(2, 2, 4, NX, ROWS, HDIM),
            *each(2, NX, ROWS, HDIM),
            pltpu.VMEM((TILES, 2, 3 * LMAX, ROWS, HDIM), jnp.float32),
            pltpu.VMEM((8, 128), jnp.int32),
            pltpu.VMEM((NX, 8, 128), jnp.int32),
            pltpu.SMEM((NX, 8, 128), jnp.int32),
            pltpu.SMEM((2, TILES), jnp.int32),
            *sems(HPD, 2, NX - 1), *sems(NX - 1), *sems(HPD, 2, NX - 1), *sems(HPD, 2, 2, 4), *sems(HPD, 2, 2, len(SPREADS)),
            *sems(HPD, NX - 1), *sems(HPD, 2, 2, len(EDGES)), *sems(HPD, 2, 2, 4), *sems(HPD, 2, NX - 1),
            pltpu.SemaphoreType.DMA((HPD, 2)),
            pltpu.SemaphoreType.DMA((HPD, 2)),
            pltpu.SemaphoreType.DMA((HPD,)),
            pltpu.SemaphoreType.DMA((HPD, 2)),
            pltpu.SemaphoreType.DMA((2,)),
        ],
        compiler_params=pltpu.CompilerParams(
            collective_id=0, has_side_effects=True, vmem_limit_bytes=48 * 2**20
        ),
        name="cross_attention_backward",
    )(q, g, k, v, lists)


def solution(mesh):
    placed = P(("grp", "seq"), None)
    return jax.shard_map(
        per_device,
        mesh=mesh,
        in_specs=(placed,) * 5,
        out_specs=(placed,) * 3,
        check_vma=False,
    )
```

```python
import jax
import jax.numpy as jnp
from jax import lax
from jax.experimental import pallas as pl
from jax.experimental.pallas import tpu as pltpu
from jax.sharding import PartitionSpec as P

MESH = pl.DeviceIdType.MESH
HEADS = 12
HDIM = 128
NX, NZ, NC = 4, 8, 8
HPD = HEADS // NX
ROWS = 32
VROWS = 256
VBLK = 128
LMAX = 8
KEYS = LMAX * ROWS
WIN = 2 * NX * NZ
TILES = 2 * NX
REACH = 2
EARLY, LATE = 0, HPD - 1
SPREADS = ((0, 5), (5, 2), (7, 1))
EDGES = ((5, 3), (0, 5))
MASKED = -1e30
LOG2E = 1.4426950408889634
BF16 = jnp.bfloat16


def dev(c, x, z):
    return {"grp": c, "seq": x * NZ + z}


def enter(c, x, z):
    barrier = pltpu.get_barrier_semaphore()

    def greet(*where):
        pl.semaphore_signal(barrier, inc=1, device_id=dev(*where), device_id_type=MESH)

    for dz in range(-REACH, REACH + 1):
        for r in range(NX):
            if dz or r:
                greet(c, (x + r) % NX, (z + dz + NZ) % NZ)

    @pl.when(c > 0)
    def _():
        greet(c - 1, x, z)

    @pl.when(c < NC - 1)
    def _():
        greet(c + 1, x, z)

    inner = jnp.logical_and(c > 0, c < NC - 1)
    pl.semaphore_wait(barrier, NX * (2 * REACH + 1) - 1 + 1 + inner.astype(jnp.int32))


def remote(src, dst, sems, at, where):
    return pltpu.make_async_remote_copy(
        src_ref=src,
        dst_ref=dst,
        send_sem=sems[0].at[at],
        recv_sem=sems[1].at[at],
        device_id=dev(*where),
        device_id_type=MESH,
    )


def at(rel):
    return NZ - 1 if abs(rel) == 4 else 2 * rel if rel >= 0 else -2 * rel - 1


def head_cols(x, h):
    return pl.ds(pl.multiple_of((x * HPD + h) * HDIM, HDIM), HDIM)


def nt(a, b):
    return lax.dot_general(a, b, (((1,), (1,)), ((), ())), preferred_element_type=jnp.float32)


def tn(a, b):
    return lax.dot_general(a, b, (((0,), (0,)), ((), ())), preferred_element_type=jnp.float32)


def nn(a, b):
    return lax.dot_general(a, b, (((1,), (0,)), ((), ())), preferred_element_type=jnp.float32)


def kernel(
    q, g, k, v, lists, out_q, out_k, out_v,
    kv0, kv1, kv2, qg0, qg1, qg2, dq0, dq1, dq2, part0, part1, part2, edge0, edge1, edge2,
    moving0, moving1, moving2, landed0, landed1, landed2, final0, final1, final2,
    pads, mine, lists_v, lists_s, runs, leaving, home,
    k_send, k_recv, i_send, i_recv, v_send, v_recv, r_send, r_recv, e_send, e_recv,
    q_send, q_recv, b_send, b_recv, s_send, s_recv, f_send, f_recv, n_send, n_recv, h_send, h_recv, own_k, own_v, own_q, own_f, own_i,
):
    c, s = lax.axis_index("grp"), lax.axis_index("seq")
    x, z = s // NZ, s % NZ
    enter(c, x, z)
    audio, video, outs = (k, v), (q, g), (out_k, out_v)
    kv, qg, dq = (kv0, kv1, kv2), (qg0, qg1, qg2), (dq0, dq1, dq2)
    part, edge = (part0, part1, part2), (edge0, edge1, edge2)
    moving, landed, final = (moving0, moving1, moving2), (landed0, landed1, landed2), (final0, final1, final2)
    above, below = jnp.minimum(c + 1, NC - 1), jnp.maximum(c - 1, 0)
    has_above, has_below = c < NC - 1, c > 0
    started, kept = [], []

    def go(copy):
        copy.start()
        started.append(copy)

    def peers():
        return [(r - 1, (x + r) % NX, (x - r + NX) % NX) for r in range(1, NX)]

    def audio_copy(h, w, r, to, came):
        return remote(audio[w].at[:, head_cols(to, h)], kv[h].at[w, 2 + came, 0], (k_send, k_recv), (h, w, r), (c, to, z))

    def video_copy(h, w, r, to, came):
        return remote(video[w].at[:, head_cols(to, h)], qg[h].at[w, came], (v_send, v_recv), (h, w, r), (c, to, z))

    def own_audio(h, w):
        return pltpu.make_async_copy(audio[w].at[:, head_cols(x, h)], kv[h].at[w, 2 + x, 0], own_k.at[h, w])

    def own_video(h, w):
        return pltpu.make_async_copy(video[w].at[:, head_cols(x, h)], qg[h].at[w, x], own_v.at[h, w])

    def list_copy(r, to, came):
        return remote(mine, lists_v.at[came], (i_send, i_recv), r, (c, to, z))

    def ring(h, w, d, step):
        sign = 1 - 2 * d
        source = kv[h].at[w, pl.ds(2, NX), at(-sign * step)]
        target = kv[h].at[w, pl.ds(2, NX), at(-sign * (step + 1))]
        return remote(source, target, (r_send, r_recv), (h, w, d, step), (c, x, (z + sign + NZ) % NZ))

    def spread_copy(h, w, d, part_of):
        low, count = SPREADS[part_of]
        span = pl.ds(low, count)
        line, there, to = ((4, 0, above), (2, 6, below))[d]
        source, target = kv[h].at[w, pl.ds(line, 2), span], kv[h].at[w, pl.ds(there, 2), span]
        return remote(source, target, (e_send, e_recv), (h, w, d, part_of), (to, x, z))

    def spread(h, w, part_of):
        @pl.when(has_above)
        def _():
            spread_copy(h, w, 0, part_of).start()

        @pl.when(has_below)
        def _():
            spread_copy(h, w, 1, part_of).start()

    def spread_wait(h, w, sent):
        for part_of in range(len(SPREADS)):

            @pl.when(has_above)
            def _():
                spread_copy(h, w, 0, part_of).wait_send() if sent else spread_copy(h, w, 1, part_of).wait_recv()

            @pl.when(has_below)
            def _():
                spread_copy(h, w, 1, part_of).wait_send() if sent else spread_copy(h, w, 0, part_of).wait_recv()

    def near_copy(w, dz, r, to, came):
        target = kv[EARLY].at[w, 2 + came, at(-dz)]
        where = (c, to, (z + dz + NZ) % NZ)
        return remote(audio[w].at[:, head_cols(to, EARLY)], target, (n_send, n_recv), (w, at(dz), r), where)

    def near_peers(dz):
        return [(r, (x + r) % NX, (x - r + NX) % NX) for r in range(NX) if dz or r]

    def relay(w, d, far):
        sign = 1 - 2 * d
        hops = 2 if far else 1
        source = kv[EARLY].at[w, pl.ds(2, NX), at(-sign * 2)]
        target = kv[EARLY].at[w, pl.ds(2, NX), at(-sign * (2 + hops))]
        return remote(source, target, (r_send, r_recv), (EARLY, w, d, hops), (c, x, (z + sign * hops + NZ) % NZ))

    for w in range(2):
        for dz in (2, -2, 1, -1, 0):
            for r, to, _ in near_peers(dz):
                go(near_copy(w, dz, r, to, x))
        own_audio(EARLY, w).start()
    for h in range(1, HPD):
        for w in range(2):
            for peer in peers():
                go(audio_copy(h, w, *peer[:2], x))
            own_audio(h, w).start()
    mine[...] = jnp.zeros_like(mine)
    mine[0:2, 0:LMAX] = lists[...]
    for peer in peers():
        go(list_copy(*peer[:2], x))
    pltpu.make_async_copy(mine, lists_v.at[x], own_i.at[0]).start()

    def send_video(h):
        for w in range(2):
            for peer in peers():
                go(video_copy(h, w, *peer[:2], x))
            own_video(h, w).start()

    send_video(EARLY)
    pads[:, :, 0:LMAX] = jnp.zeros((TILES, 2, LMAX, ROWS, HDIM), jnp.float32)
    pads[:, :, 2 * LMAX : 3 * LMAX] = jnp.zeros((TILES, 2, LMAX, ROWS, HDIM), jnp.float32)
    for h in range(HPD):

        @pl.when(c == 0)
        def _():
            edge[h][:, 0] = jnp.zeros((2,) + edge[h].shape[2:], BF16)

        @pl.when(c == NC - 1)
        def _():
            edge[h][:, 1] = jnp.zeros((2,) + edge[h].shape[2:], BF16)

    def near_in(w, dz):
        for r, to, came in near_peers(dz):
            near_copy(w, dz, r, to, came).wait_recv()

    def first_step(h):
        for w in range(2):
            own_audio(h, w).wait()
            for peer in peers():
                audio_copy(h, w, *peer).wait_recv()
            for d in range(2):
                go(ring(h, w, d, 0))

    def next_step(h, step):
        for w in range(2):
            for d in range(2):
                if step == 4 and w != d:
                    continue
                ring(h, w, d, step - 1).wait_recv()
                if step < 3 or (step == 3 and w == d):
                    go(ring(h, w, d, step))
            if step > 1:
                spread(h, w, step - 2)

    for w in range(2):
        for d in range(2):
            near_in(w, 2 - 4 * d)
            go(relay(w, d, False))
            if w == d:
                go(relay(w, d, True))
    for h in range(1, HPD):
        first_step(h)
    for w in range(2):
        own_audio(EARLY, w).wait()
        for dz in (0, 1, -1):
            near_in(w, dz)
        spread(EARLY, w, 0)
    for h in range(1, HPD):
        next_step(h, 1)
    send_video(1)
    for w in range(2):
        for d in range(2):
            relay(w, d, False).wait_recv()
        relay(w, w, True).wait_recv()
        spread(EARLY, w, 1)
        spread(EARLY, w, 2)

    pltpu.make_async_copy(mine, lists_v.at[x], own_i.at[0]).wait()
    for peer in peers():
        list_copy(*peer).wait_recv()
    fetched = pltpu.make_async_copy(lists_v, lists_s, own_i.at[1])
    fetched.start()
    fetched.wait()
    for t in range(TILES):
        count = jnp.int32(0)
        for j in range(LMAX):
            count += (lists_s[t // 2, t % 2, j] >= 0).astype(jnp.int32)
        runs[0, t] = jnp.clip(lists_s[t // 2, t % 2, 0] - (c * NX * NZ - NX * NZ // 2), 0, WIN - 1)
        runs[1, t] = count

    scale = HDIM**-0.5

    def tiles(h):
        loaded, ready_terms = [], []
        for t in range(TILES):
            first, count = runs[0, t], runs[1, t]
            blocks = [jnp.minimum(first + jnp.where(j < count, j, 0), WIN - 1) for j in range(LMAX)]
            places = [(e >> 3, ((e & 7) - z + NZ) & 7) for e in blocks]
            places = [(line, jnp.where(rel < 4, 2 * rel, 15 - 2 * rel)) for line, rel in places]
            kt = jnp.concatenate([kv[h][0, line, where] for line, where in places], axis=0)
            vt = jnp.concatenate([kv[h][1, line, where] for line, where in places], axis=0)
            rows = pl.ds(t % 2 * VBLK, VBLK)
            qt, gt = qg[h][0, t // 2, rows], qg[h][1, t // 2, rows]
            loaded.append((count, kt, qt, gt, nt(kt, qt), nt(vt, gt)))
        for count, kt, qt, gt, products, grad_weights in loaded:
            dead = [jnp.full((ROWS, VBLK), jnp.where(j < count, 0.0, MASKED), jnp.float32) for j in range(LMAX)]
            scores = products * (scale * LOG2E) + jnp.concatenate(dead, axis=0)
            raw = jnp.exp2(scores - jnp.max(scores, axis=0, keepdims=True))
            inverse = 1.0 / jnp.sum(raw, axis=0, keepdims=True)
            inner = jnp.sum(raw * grad_weights, axis=0, keepdims=True) * inverse
            weights_low = (raw * inverse).astype(BF16)
            grad_scores = (raw * ((grad_weights - inner) * (inverse * scale))).astype(BF16)
            ready_terms.append((kt, qt, gt, weights_low, grad_scores))
        for t, (kt, qt, gt, weights_low, grad_scores) in enumerate(ready_terms):
            pads[t, 1, LMAX : 2 * LMAX] = nn(weights_low, gt).reshape(LMAX, ROWS, HDIM)
            pads[t, 0, LMAX : 2 * LMAX] = nn(grad_scores, qt).reshape(LMAX, ROWS, HDIM)
            dq[h][t // 2, pl.ds(t % 2 * VBLK, VBLK)] = tn(grad_scores, kt).astype(BF16)

    def place(h):
        for w in range(2):
            for line in range(2 * NX):
                near = range(max(0, line - NX) * 2, min(NX, line + 1) * 2)
                total = None
                for t in near:
                    term = pads[t, w, pl.ds(jnp.clip(line * NZ - runs[0, t] + LMAX, 0, 2 * LMAX), LMAX)]
                    total = term if total is None else total + term
                total = total.astype(BF16)
                for zz in range(NZ):
                    rel = (zz - z + NZ) & 7
                    part[h][w, line, jnp.where(rel < 4, 2 * rel, 15 - 2 * rel)] = total[zz]

    def query_copy(h, r, to, mine_at):
        return remote(dq[h].at[to], out_q.at[:, head_cols(mine_at, h)], (q_send, q_recv), (h, r), (c, to, z))

    def own_query(h):
        return pltpu.make_async_copy(dq[h].at[x], out_q.at[:, head_cols(x, h)], own_q.at[h])

    def edge_copy(h, w, d, part_of):
        low, count = EDGES[part_of]
        line, to = ((6, above), (0, below))[d]
        source, target = part[h].at[w, pl.ds(line, 2), pl.ds(low, count)], edge[h].at[w, d, :, pl.ds(low, count)]
        return remote(source, target, (b_send, b_recv), (h, w, d, part_of), (to, x, z))

    def hand_out(h):
        for part_of in range(len(EDGES)):
            for w in range(2):

                @pl.when(has_above)
                def _():
                    edge_copy(h, w, 0, part_of).start()

                @pl.when(has_below)
                def _():
                    edge_copy(h, w, 1, part_of).start()

        for peer in peers():
            go(query_copy(h, *peer[:2], x))
        own_query(h).start()

    def edges_in(h, w, part_of):
        @pl.when(has_above)
        def _():
            edge_copy(h, w, 1, part_of).wait_recv()

        @pl.when(has_below)
        def _():
            edge_copy(h, w, 0, part_of).wait_recv()

    def total(h, w, rel):
        p = at(rel)
        low = part[h][w, 2:4, p].astype(jnp.float32) + edge[h][w, 0, :, p].astype(jnp.float32)
        high = part[h][w, 4:6, p].astype(jnp.float32) + edge[h][w, 1, :, p].astype(jnp.float32)
        return jnp.concatenate([low, high], axis=0)

    def sum_ring(h, w, d, dist):
        slot = (w, d, dist - 1)
        return remote(moving[h].at[slot], landed[h].at[slot], (s_send, s_recv), (h, *slot), (c, x, (z + 1 - 2 * d + NZ) % NZ))

    def sums(h, dist):
        for w in range(2):
            if dist in (4, 2):
                edges_in(h, w, 0 if dist == 4 else 1)
            for d in range(2):
                if dist == 4 and w != d:
                    continue
                value = total(h, w, -dist if d else dist)
                if dist < 3 or (dist == 3 and w == d):
                    sum_ring(h, w, d, dist + 1).wait_recv()
                    value = value + landed[h][w, d, dist].astype(jnp.float32)
                moving[h][w, d, dist - 1] = value.astype(BF16)
                go(sum_ring(h, w, d, dist))

    def final_copy(h, w, r, to, mine_at):
        return remote(final[h].at[w, to], outs[w].at[:, head_cols(mine_at, h)], (f_send, f_recv), (h, w, r), (c, to, z))

    def own_final(h, w):
        return pltpu.make_async_copy(final[h].at[w, x], outs[w].at[:, head_cols(x, h)], own_f.at[h, w, 0])

    def finish(h):
        for w in range(2):
            value = total(h, w, 0)
            for d in range(2):
                sum_ring(h, w, d, 1).wait_recv()
                value = value + landed[h][w, d, 0].astype(jnp.float32)
            final[h][w] = value.astype(BF16)
            for peer in peers():
                go(final_copy(h, w, *peer[:2], x))
            own_final(h, w).start()

    def ready(h):
        for w in range(2):
            spread_wait(h, w, False)
            own_video(h, w).wait()
            for peer in peers():
                video_copy(h, w, *peer).wait_recv()

    def compute(h):
        ready(h)
        tiles(h)
        place(h)
        hand_out(h)

    def home_copy(w, rel, r, to, mine_at):
        where = (c, to, (z + rel + NZ) % NZ)
        return remote(leaving.at[w, at(rel), to], home.at[w, mine_at, at(-rel)], (h_send, h_recv), (w, at(rel), r), where)

    def send_home(w, rel, value):
        leaving[w, at(rel)] = value.astype(BF16)
        for r, to, _ in near_peers(rel):
            go(home_copy(w, rel, r, to, x))
        if rel == 0:
            home[w, x, 0] = leaving[w, 0, x]

    def last_ring(w, d, dist):
        sign, slot = 1 - 2 * d, (w, d, dist - 1)
        where = (c, x, (z + sign * (dist - 2) + NZ) % NZ)
        return remote(moving[LATE].at[slot], landed[LATE].at[slot], (s_send, s_recv), (LATE, *slot), where)

    def last_far():
        for w in range(2):
            edges_in(LATE, w, 0)
            for dist in (4, 3):
                for d in range(2):
                    if dist == 3 or w == d:
                        moving[LATE][w, d, dist - 1] = total(LATE, w, -dist if d else dist).astype(BF16)
                        go(last_ring(w, d, dist))

    def last_near():
        for w in range(2):
            edges_in(LATE, w, 1)
            for rel in (1, -1, 0):
                send_home(w, rel, total(LATE, w, rel))

    def last_two():
        for w in range(2):
            for d in range(2):
                rel = -2 if d else 2
                last_ring(w, d, 3).wait_recv()
                value = total(LATE, w, rel) + landed[LATE][w, d, 2].astype(jnp.float32)
                if w == d:
                    last_ring(w, d, 4).wait_recv()
                    value = value + landed[LATE][w, d, 3].astype(jnp.float32)
                send_home(w, rel, value)

    def own_last(w, line):
        return pltpu.make_async_copy(final[LATE].at[w, line], outs[w].at[:, head_cols(line, LATE)], own_f.at[LATE, w, line])

    def last_finish():
        for w in range(2):
            for rel in (0, 1, -1, 2, -2):
                for r, to, came in near_peers(rel):
                    home_copy(w, rel, r, to, came).wait_recv()
            value = home[w, :, 0].astype(jnp.float32)
            for i in range(1, 2 * REACH + 1):
                value = value + home[w, :, i].astype(jnp.float32)
            final[LATE][w] = value.astype(BF16)
            for line in range(NX):
                own_last(w, line).start()

    def steps(step):
        for h in range(1, HPD):
            next_step(h, step)

    steps(2)
    compute(0)
    send_video(2)
    steps(3)
    sums(0, 4)
    steps(4)
    sums(0, 3)
    compute(1)
    sums(0, 2)
    compute(2)
    sums(1, 4)
    sums(0, 1)
    sums(1, 3)
    last_far()
    finish(0)
    sums(1, 2)
    last_near()
    last_two()
    sums(1, 1)
    finish(1)
    last_finish()

    for h in range(HPD):
        own_query(h).wait()
        for peer in peers():
            r, to, came = peer
            query_copy(h, r, to, came).wait_recv()
        for w in range(2):
            spread_wait(h, w, True)
            if h == LATE:
                for line in range(NX):
                    own_last(w, line).wait()
            else:
                own_final(h, w).wait()
                for r, to, came in peers():
                    final_copy(h, w, r, to, came).wait_recv()

            for part_of in range(len(EDGES)):

                @pl.when(has_above)
                def _():
                    edge_copy(h, w, 0, part_of).wait_send()

                @pl.when(has_below)
                def _():
                    edge_copy(h, w, 1, part_of).wait_send()

    for copy in started:
        copy.wait_send()


HBM = pl.BlockSpec(memory_space=pltpu.HBM)
VMEM = pl.BlockSpec(memory_space=pltpu.VMEM)


def sems(*shape):
    return [pltpu.SemaphoreType.DMA(shape)] * 2


def each(*shape):
    return [pltpu.VMEM(shape, BF16)] * HPD


def per_device(q, k, v, g, lists):
    return pl.pallas_call(
        kernel,
        out_shape=tuple(jax.ShapeDtypeStruct(a.shape, BF16) for a in (q, k, v)),
        in_specs=[HBM] * 4 + [VMEM],
        out_specs=(HBM,) * 3,
        scratch_shapes=[
            *each(2, 2 * NX, NZ, ROWS, HDIM),
            *each(2, NX, VROWS, HDIM),
            *each(NX, VROWS, HDIM),
            *each(2, 2 * NX, NZ, ROWS, HDIM),
            *each(2, 2, 2, NZ, ROWS, HDIM),
            *each(2, 2, 4, NX, ROWS, HDIM),
            *each(2, 2, 4, NX, ROWS, HDIM),
            *each(2, NX, ROWS, HDIM),
            pltpu.VMEM((TILES, 2, 3 * LMAX, ROWS, HDIM), jnp.float32),
            pltpu.VMEM((8, 128), jnp.int32),
            pltpu.VMEM((NX, 8, 128), jnp.int32),
            pltpu.SMEM((NX, 8, 128), jnp.int32),
            pltpu.SMEM((2, TILES), jnp.int32),
            pltpu.VMEM((2, 2 * REACH + 1, NX, ROWS, HDIM), BF16),
            pltpu.VMEM((2, NX, 2 * REACH + 1, ROWS, HDIM), BF16),
            *sems(HPD, 2, NX - 1), *sems(NX - 1), *sems(HPD, 2, NX - 1), *sems(HPD, 2, 2, 4), *sems(HPD, 2, 2, len(SPREADS)),
            *sems(HPD, NX - 1), *sems(HPD, 2, 2, len(EDGES)), *sems(HPD, 2, 2, 4), *sems(HPD, 2, NX - 1),
            *sems(2, 2 * REACH + 1, NX), *sems(2, 2 * REACH + 1, NX),
            pltpu.SemaphoreType.DMA((HPD, 2)),
            pltpu.SemaphoreType.DMA((HPD, 2)),
            pltpu.SemaphoreType.DMA((HPD,)),
            pltpu.SemaphoreType.DMA((HPD, 2, NX)),
            pltpu.SemaphoreType.DMA((2,)),
        ],
        compiler_params=pltpu.CompilerParams(
            collective_id=0, has_side_effects=True, vmem_limit_bytes=62 * 2**20
        ),
        name="cross_attention_backward",
    )(q, g, k, v, lists)


def solution(mesh):
    placed = P(("grp", "seq"), None)
    return jax.shard_map(
        per_device,
        mesh=mesh,
        in_specs=(placed,) * 5,
        out_specs=(placed,) * 3,
        check_vma=False,
    )
```

```python
import jax
import jax.numpy as jnp
from jax import lax
from jax.experimental import pallas as pl
from jax.experimental.pallas import tpu as pltpu
from jax.sharding import PartitionSpec as P

MESH = pl.DeviceIdType.MESH
HEADS = 12
HDIM = 128
NX, NZ, NC = 4, 8, 8
HPD = HEADS // NX
ROWS = 32
VROWS = 256
VBLK = 128
LMAX = 8
KEYS = LMAX * ROWS
WIN = 2 * NX * NZ
TILES = 2 * NX
REACH = 2
EARLY, LATE = 0, HPD - 1
SPREADS = ((0, 5), (5, 2), (7, 1))
EDGES = ((5, 3), (0, 5))
MASKED = -1e30
LOG2E = 1.4426950408889634
BF16 = jnp.bfloat16


def dev(c, x, z):
    return {"grp": c, "seq": x * NZ + z}


def enter(c, x, z):
    barrier = pltpu.get_barrier_semaphore()

    def greet(*where):
        pl.semaphore_signal(barrier, inc=1, device_id=dev(*where), device_id_type=MESH)

    for dz in range(-REACH, REACH + 1):
        for r in range(NX):
            if dz or r:
                greet(c, (x + r) % NX, (z + dz + NZ) % NZ)

    @pl.when(c > 0)
    def _():
        greet(c - 1, x, z)

    @pl.when(c < NC - 1)
    def _():
        greet(c + 1, x, z)

    inner = jnp.logical_and(c > 0, c < NC - 1)
    pl.semaphore_wait(barrier, NX * (2 * REACH + 1) - 1 + 1 + inner.astype(jnp.int32))


def remote(src, dst, send, recv, where):
    return pltpu.make_async_remote_copy(
        src_ref=src, dst_ref=dst, send_sem=send, recv_sem=recv, device_id=dev(*where), device_id_type=MESH
    )


def local(src, dst, sem):
    return pltpu.make_async_copy(src, dst, sem)


def at(rel):
    return NZ - 1 if abs(rel) == 4 else 2 * rel if rel >= 0 else -2 * rel - 1


def head_cols(x, h):
    return pl.ds(pl.multiple_of((x * HPD + h) * HDIM, HDIM), HDIM)


def nt(a, b):
    return lax.dot_general(a, b, (((1,), (1,)), ((), ())), preferred_element_type=jnp.float32)


def tn(a, b):
    return lax.dot_general(a, b, (((0,), (0,)), ((), ())), preferred_element_type=jnp.float32)


def nn(a, b):
    return lax.dot_general(a, b, (((1,), (0,)), ((), ())), preferred_element_type=jnp.float32)


def kernel(
    q, g, k, v, lists, out_q, out_k, out_v,
    kv0, kv1, kv2, qg0, qg1, qg2, dq0, dq1, dq2, part0, part1, part2, edge0, edge1, edge2,
    moving0, moving1, moving2, landed0, landed1, landed2, final0, final1, final2,
    pads, mine, lists_v, lists_s, runs, leaving, home,
    sent, up_sent, down_sent, near_sem, audio_sem, video_sem, ring_sem, spread_sem, edge_sem, sum_sem, out_sem, home_sem, list_sem,
):
    c, s = lax.axis_index("grp"), lax.axis_index("seq")
    x, z = s // NZ, s % NZ
    enter(c, x, z)
    audio, video, outs = (k, v), (q, g), (out_k, out_v)
    kv, qg, dq = (kv0, kv1, kv2), (qg0, qg1, qg2), (dq0, dq1, dq2)
    part, edge = (part0, part1, part2), (edge0, edge1, edge2)
    moving, landed, final = (moving0, moving1, moving2), (landed0, landed1, landed2), (final0, final1, final2)
    above, below = jnp.minimum(c + 1, NC - 1), jnp.maximum(c - 1, 0)
    has_above, has_below = c < NC - 1, c > 0
    NEAR, AUDIO, VIDEO, LIST, RING, SUM, QUERY, FINAL, HOME = (sent.at[i] for i in range(9))

    def awaited(ref, sem):
        local(ref, ref, sem).wait()

    def peers():
        return [(x + r) % NX for r in range(1, NX)]

    def along(sign, hops):
        return (c, x, (z + sign * hops + NZ) % NZ)

    def send_near():
        for w in range(2):
            for dz in (2, -2, 1, -1, 0):
                for r in range(NX):
                    to = (x + r) % NX
                    source, target = audio[w].at[:, head_cols(to, EARLY)], kv[EARLY].at[w, 2 + x, at(-dz)]
                    if dz or r:
                        remote(source, target, NEAR, near_sem.at[at(dz)], (c, to, (z + dz + NZ) % NZ)).start()
                    else:
                        local(source, target, near_sem.at[0]).start()

    def near_in(dz):
        awaited(kv[EARLY].at[:, pl.ds(2, NX), at(-dz)], near_sem.at[at(dz)])

    def send_audio(h):
        for w in range(2):
            for to in peers():
                source, target = audio[w].at[:, head_cols(to, h)], kv[h].at[w, 2 + x, 0]
                remote(source, target, AUDIO, audio_sem.at[h], (c, to, z)).start()
            local(audio[w].at[:, head_cols(x, h)], kv[h].at[w, 2 + x, 0], audio_sem.at[h]).start()

    def send_video(h):
        for w in range(2):
            for to in peers():
                source, target = video[w].at[:, head_cols(to, h)], qg[h].at[w, x]
                remote(source, target, VIDEO, video_sem.at[h], (c, to, z)).start()
            local(video[w].at[:, head_cols(x, h)], qg[h].at[w, x], video_sem.at[h]).start()

    def onward(h, d, far, hops, slot, whole):
        sign = 1 - 2 * d
        what = pl.ds(0, 2) if whole else pl.ds(d, 1)
        source = kv[h].at[what, pl.ds(2, NX), at(-sign * far)]
        target = kv[h].at[what, pl.ds(2, NX), at(-sign * (far + hops))]
        return remote(source, target, RING, ring_sem.at[h, d, slot], along(sign, hops))

    def spread(h, low, count):
        span = pl.ds(low, count)

        @pl.when(has_above)
        def _():
            source, target = kv[h].at[:, pl.ds(4, 2), span], kv[h].at[:, pl.ds(0, 2), span]
            remote(source, target, up_sent.at[0], spread_sem.at[h, 0], (above, x, z)).start()

        @pl.when(has_below)
        def _():
            source, target = kv[h].at[:, pl.ds(2, 2), span], kv[h].at[:, pl.ds(6, 2), span]
            remote(source, target, down_sent.at[0], spread_sem.at[h, 1], (below, x, z)).start()

    def ready(h):
        awaited(qg[h], video_sem.at[h])

        @pl.when(has_above)
        def _():
            awaited(kv[h].at[:, pl.ds(6, 2)], spread_sem.at[h, 1])

        @pl.when(has_below)
        def _():
            awaited(kv[h].at[:, pl.ds(0, 2)], spread_sem.at[h, 0])

    def first_step(h):
        awaited(kv[h].at[:, pl.ds(2, NX), 0], audio_sem.at[h])
        for d in range(2):
            onward(h, d, 0, 1, 0, True).start()

    def next_step(h, step):
        for d in range(2):
            onward(h, d, step - 1, 1, step - 1, step < 4).wait_recv()
            if step < 4:
                onward(h, d, step, 1, step, step < 3).start()
        if step > 1:
            spread(h, *SPREADS[step - 2])

    send_near()
    for h in range(1, HPD):
        send_audio(h)
    mine[...] = jnp.zeros_like(mine)
    mine[0:2, 0:LMAX] = lists[...]
    for to in peers():
        remote(mine, lists_v.at[x], LIST, list_sem.at[0], (c, to, z)).start()
    local(mine, lists_v.at[x], list_sem.at[0]).start()
    send_video(EARLY)
    pads[:, :, 0:LMAX] = jnp.zeros((TILES, 2, LMAX, ROWS, HDIM), jnp.float32)
    pads[:, :, 2 * LMAX : 3 * LMAX] = jnp.zeros((TILES, 2, LMAX, ROWS, HDIM), jnp.float32)
    for h in range(HPD):

        @pl.when(c == 0)
        def _():
            edge[h][:, 0] = jnp.zeros((2,) + edge[h].shape[2:], BF16)

        @pl.when(c == NC - 1)
        def _():
            edge[h][:, 1] = jnp.zeros((2,) + edge[h].shape[2:], BF16)

    for d in range(2):
        near_in(2 - 4 * d)
        onward(EARLY, d, 2, 1, 0, True).start()
        onward(EARLY, d, 2, 2, 1, False).start()
    for h in range(1, HPD):
        first_step(h)
    for dz in (0, 1, -1):
        near_in(dz)
    spread(EARLY, 0, 5)
    for h in range(1, HPD):
        next_step(h, 1)
    send_video(1)
    for d in range(2):
        onward(EARLY, d, 2, 1, 0, True).wait_recv()
        onward(EARLY, d, 2, 2, 1, False).wait_recv()
    spread(EARLY, 5, 3)

    awaited(lists_v, list_sem.at[0])
    fetched = local(lists_v, lists_s, list_sem.at[1])
    fetched.start()
    fetched.wait()
    for t in range(TILES):
        count = jnp.int32(0)
        for j in range(LMAX):
            count += (lists_s[t // 2, t % 2, j] >= 0).astype(jnp.int32)
        runs[0, t] = jnp.clip(lists_s[t // 2, t % 2, 0] - (c * NX * NZ - NX * NZ // 2), 0, WIN - 1)
        runs[1, t] = count

    scale = HDIM**-0.5

    def tiles(h):
        loaded, ready_terms = [], []
        for t in range(TILES):
            first, count = runs[0, t], runs[1, t]
            blocks = [jnp.minimum(first + jnp.where(j < count, j, 0), WIN - 1) for j in range(LMAX)]
            places = [(e >> 3, ((e & 7) - z + NZ) & 7) for e in blocks]
            places = [(line, jnp.where(rel < 4, 2 * rel, 15 - 2 * rel)) for line, rel in places]
            kt = jnp.concatenate([kv[h][0, line, where] for line, where in places], axis=0)
            vt = jnp.concatenate([kv[h][1, line, where] for line, where in places], axis=0)
            rows = pl.ds(t % 2 * VBLK, VBLK)
            qt, gt = qg[h][0, t // 2, rows], qg[h][1, t // 2, rows]
            loaded.append((count, kt, qt, gt, nt(kt, qt), nt(vt, gt)))
        for count, kt, qt, gt, products, grad_weights in loaded:
            dead = [jnp.full((ROWS, VBLK), jnp.where(j < count, 0.0, MASKED), jnp.float32) for j in range(LMAX)]
            scores = products * (scale * LOG2E) + jnp.concatenate(dead, axis=0)
            raw = jnp.exp2(scores - jnp.max(scores, axis=0, keepdims=True))
            inverse = 1.0 / jnp.sum(raw, axis=0, keepdims=True)
            inner = jnp.sum(raw * grad_weights, axis=0, keepdims=True) * inverse
            weights_low = (raw * inverse).astype(BF16)
            grad_scores = (raw * ((grad_weights - inner) * (inverse * scale))).astype(BF16)
            ready_terms.append((kt, qt, gt, weights_low, grad_scores))
        for t, (kt, qt, gt, weights_low, grad_scores) in enumerate(ready_terms):
            pads[t, 1, LMAX : 2 * LMAX] = nn(weights_low, gt).reshape(LMAX, ROWS, HDIM)
            pads[t, 0, LMAX : 2 * LMAX] = nn(grad_scores, qt).reshape(LMAX, ROWS, HDIM)
            dq[h][t // 2, pl.ds(t % 2 * VBLK, VBLK)] = tn(grad_scores, kt).astype(BF16)

    def place(h):
        for w in range(2):
            for line in range(2 * NX):
                near = range(max(0, line - NX) * 2, min(NX, line + 1) * 2)
                total = None
                for t in near:
                    term = pads[t, w, pl.ds(jnp.clip(line * NZ - runs[0, t] + LMAX, 0, 2 * LMAX), LMAX)]
                    total = term if total is None else total + term
                total = total.astype(BF16)
                for zz in range(NZ):
                    rel = (zz - z + NZ) & 7
                    part[h][w, line, jnp.where(rel < 4, 2 * rel, 15 - 2 * rel)] = total[zz]

    def edge_copy(h, d, part_of):
        low, count = EDGES[part_of]
        line, to, sem = ((6, above, up_sent), (0, below, down_sent))[d]
        source, target = part[h].at[:, pl.ds(line, 2), pl.ds(low, count)], edge[h].at[:, d, :, pl.ds(low, count)]
        return remote(source, target, sem.at[1], edge_sem.at[h, d, part_of], (to, x, z))

    def hand_out(h):
        for part_of in range(len(EDGES)):

            @pl.when(has_above)
            def _():
                edge_copy(h, 0, part_of).start()

            @pl.when(has_below)
            def _():
                edge_copy(h, 1, part_of).start()

        for to in peers():
            remote(dq[h].at[to], out_q.at[:, head_cols(x, h)], QUERY, out_sem.at[2], (c, to, z)).start()
        local(dq[h].at[x], out_q.at[:, head_cols(x, h)], out_sem.at[2]).start()

    def edges_in(h, part_of):
        @pl.when(has_above)
        def _():
            edge_copy(h, 1, part_of).wait_recv()

        @pl.when(has_below)
        def _():
            edge_copy(h, 0, part_of).wait_recv()

    def total(h, w, rel):
        p = at(rel)
        low = part[h][w, 2:4, p].astype(jnp.float32) + edge[h][w, 0, :, p].astype(jnp.float32)
        high = part[h][w, 4:6, p].astype(jnp.float32) + edge[h][w, 1, :, p].astype(jnp.float32)
        return jnp.concatenate([low, high], axis=0)

    def sum_copy(h, d, dist, hops):
        what = pl.ds(0, 2) if dist < 4 else pl.ds(d, 1)
        source, target = moving[h].at[d, dist - 1, what], landed[h].at[d, dist - 1, what]
        return remote(source, target, SUM, sum_sem.at[h, d, dist - 1], along(1 - 2 * d, hops))

    def sums(h, dist):
        if dist in (4, 2):
            edges_in(h, 0 if dist == 4 else 1)
        for d in range(2):
            if dist < 4:
                sum_copy(h, d, dist + 1, 1).wait_recv()
            for w in range(2):
                if dist == 4 and w != d:
                    continue
                value = total(h, w, -dist if d else dist)
                if dist < 3 or (dist == 3 and w == d):
                    value = value + landed[h][d, dist, w].astype(jnp.float32)
                moving[h][d, dist - 1, w] = value.astype(BF16)
            sum_copy(h, d, dist, 1).start()

    def finish(h):
        for d in range(2):
            sum_copy(h, d, 1, 1).wait_recv()
        for w in range(2):
            value = total(h, w, 0)
            for d in range(2):
                value = value + landed[h][d, 0, w].astype(jnp.float32)
            final[h][w] = value.astype(BF16)
            target = outs[w].at[:, head_cols(x, h)]
            for to in peers():
                remote(final[h].at[w, to], target, FINAL, out_sem.at[w], (c, to, z)).start()
            local(final[h].at[w, x], target, out_sem.at[w]).start()

    def send_home(w, rel, value):
        leaving[w, at(rel)] = value.astype(BF16)
        for r in range(NX):
            to = (x + r) % NX
            source, target = leaving.at[w, at(rel), to], home.at[w, x, at(-rel)]
            if rel or r:
                remote(source, target, HOME, home_sem.at[0], (c, to, (z + rel + NZ) % NZ)).start()
            else:
                local(source, target, home_sem.at[0]).start()

    def last_far():
        edges_in(LATE, 0)
        for dist in (4, 3):
            for d in range(2):
                for w in range(2):
                    if dist == 3 or w == d:
                        moving[LATE][d, dist - 1, w] = total(LATE, w, -dist if d else dist).astype(BF16)
                sum_copy(LATE, d, dist, dist - 2).start()

    def last_near():
        edges_in(LATE, 1)
        for w in range(2):
            for rel in (1, -1, 0):
                send_home(w, rel, total(LATE, w, rel))

    def last_two():
        for d in range(2):
            for dist in (3, 4):
                sum_copy(LATE, d, dist, dist - 2).wait_recv()
            for w in range(2):
                rel = -2 if d else 2
                value = total(LATE, w, rel) + landed[LATE][d, 2, w].astype(jnp.float32)
                if w == d:
                    value = value + landed[LATE][d, 3, w].astype(jnp.float32)
                send_home(w, rel, value)

    def last_finish():
        awaited(home, home_sem.at[0])
        for w in range(2):
            value = home[w, :, 0].astype(jnp.float32)
            for i in range(1, 2 * REACH + 1):
                value = value + home[w, :, i].astype(jnp.float32)
            final[LATE][w] = value.astype(BF16)
            for line in range(NX):
                local(final[LATE].at[w, line], outs[w].at[:, head_cols(line, LATE)], out_sem.at[w]).start()

    def compute(h):
        ready(h)
        tiles(h)
        place(h)
        hand_out(h)

    def steps(step):
        for h in range(1, HPD):
            next_step(h, step)

    steps(2)
    compute(0)
    send_video(2)
    steps(3)
    sums(0, 4)
    steps(4)
    sums(0, 3)
    compute(1)
    sums(0, 2)
    compute(2)
    sums(1, 4)
    sums(0, 1)
    sums(1, 3)
    last_far()
    finish(0)
    sums(1, 2)
    last_near()
    last_two()
    sums(1, 1)
    finish(1)
    last_finish()

    awaited(out_q, out_sem.at[2])
    for w in range(2):
        awaited(outs[w], out_sem.at[w])
    for i in range(2):

        @pl.when(has_above)
        def _():
            awaited(pads.at[pl.ds(0, 2), 0], up_sent.at[i])

        @pl.when(has_below)
        def _():
            awaited(pads.at[pl.ds(0, 2), 0], down_sent.at[i])

    for sem, a, b in ((NEAR, 1, 19), (AUDIO, 1, 6), (VIDEO, 3, 24), (RING, 4, 17), (SUM, 4, 17), (QUERY, 3, 12), (FINAL, 1, 6), (HOME, 1, 19)):
        awaited(pads.at[pl.ds(0, a), 0, pl.ds(0, b)], sem)
    awaited(lists_v.at[pl.ds(0, NX - 1)], LIST)


HBM = pl.BlockSpec(memory_space=pltpu.HBM)
VMEM = pl.BlockSpec(memory_space=pltpu.VMEM)


def sems(*shape):
    return pltpu.SemaphoreType.DMA(shape)


def each(*shape):
    return [pltpu.VMEM(shape, BF16)] * HPD


def per_device(q, k, v, g, lists):
    return pl.pallas_call(
        kernel,
        out_shape=tuple(jax.ShapeDtypeStruct(a.shape, BF16) for a in (q, k, v)),
        in_specs=[HBM] * 4 + [VMEM],
        out_specs=(HBM,) * 3,
        scratch_shapes=[
            *each(2, 2 * NX, NZ, ROWS, HDIM),
            *each(2, NX, VROWS, HDIM),
            *each(NX, VROWS, HDIM),
            *each(2, 2 * NX, NZ, ROWS, HDIM),
            *each(2, 2, 2, NZ, ROWS, HDIM),
            *each(2, 4, 2, NX, ROWS, HDIM),
            *each(2, 4, 2, NX, ROWS, HDIM),
            *each(2, NX, ROWS, HDIM),
            pltpu.VMEM((TILES, 2, 3 * LMAX, ROWS, HDIM), jnp.float32),
            pltpu.VMEM((8, 128), jnp.int32),
            pltpu.VMEM((NX, 8, 128), jnp.int32),
            pltpu.SMEM((NX, 8, 128), jnp.int32),
            pltpu.SMEM((2, TILES), jnp.int32),
            pltpu.VMEM((2, 2 * REACH + 1, NX, ROWS, HDIM), BF16),
            pltpu.VMEM((2, NX, 2 * REACH + 1, ROWS, HDIM), BF16),
            sems(9), sems(2), sems(2), sems(2 * REACH + 1), sems(HPD), sems(HPD), sems(HPD, 2, 4), sems(HPD, 2),
            sems(HPD, 2, len(EDGES)), sems(HPD, 2, 4), sems(3), sems(1), sems(2),
        ],
        compiler_params=pltpu.CompilerParams(
            collective_id=0, has_side_effects=True, vmem_limit_bytes=62 * 2**20
        ),
        name="cross_attention_backward",
    )(q, g, k, v, lists)


def solution(mesh):
    placed = P(("grp", "seq"), None)
    return jax.shard_map(
        per_device,
        mesh=mesh,
        in_specs=(placed,) * 5,
        out_specs=(placed,) * 3,
        check_vma=False,
    )
```

```python
import jax
import jax.numpy as jnp
from jax import lax
from jax.experimental import pallas as pl
from jax.experimental.pallas import tpu as pltpu
from jax.sharding import PartitionSpec as P

MESH = pl.DeviceIdType.MESH
HEADS = 12
HDIM = 128
NX, NZ, NC = 4, 8, 8
HPD = HEADS // NX
ROWS = 32
VROWS = 256
VBLK = 128
LMAX = 8
KEYS = LMAX * ROWS
WIN = 2 * NX * NZ
TILES = 2 * NX
LATE = HPD - 1
HOMING = True
PIECES = ((0, 2),)
SPREADS = ((0, 5), (5, 2), (7, 1))
EDGES = ((7, 1), (5, 2), (0, 5))
MASKED = -1e30
LOG2E = 1.4426950408889634
BF16 = jnp.bfloat16


SCHEDULE = (
    ("audio", 0), ("audio", 1), ("audio", 2), ("lists",), ("video", 0),
    ("there", 0, 0), ("there", 1, 0), ("there", 2, 0), ("clear",), ("there", 0, 1), ("there", 1, 1), ("there", 2, 1),
    ("video", 1), ("there", 0, 2), ("there", 1, 2), ("there", 2, 2), ("video", 2), ("there", 0, 3), ("there", 1, 3),
    ("there", 2, 3), ("read",), ("there", 0, 4), ("there", 1, 4), ("there", 2, 4),
    ("compute", 0), ("compute", 1), ("compute", 2), ("edges", 0), ("edges", 1), ("edges", 2),
    ("back", 0, 4), ("back", 1, 4), ("back", 2, 4),
    ("back", 0, 3), ("back", 1, 3), ("back", 2, 3), ("back", 0, 2), ("back", 1, 2), ("back", 2, 2),
    ("back", 0, 1), ("back", 1, 1), ("back", 2, 1), ("back", 0, 0), ("back", 1, 0), ("back", 2, 0),
)


def dev(c, x, z):
    return {"grp": c, "seq": x * NZ + z}


def enter(c, x, z):
    barrier = pltpu.get_barrier_semaphore()

    def greet(*where):
        pl.semaphore_signal(barrier, inc=1, device_id=dev(*where), device_id_type=MESH)

    peers = [(r, dz) for dz in (-1, 0, 1) for r in range(NX) if (r or dz) and (HOMING or not r or not dz)]
    for r, dz in peers:
        greet(c, (x + r) % NX, (z + dz + NZ) % NZ)

    @pl.when(c > 0)
    def _():
        greet(c - 1, x, z)

    @pl.when(c < NC - 1)
    def _():
        greet(c + 1, x, z)

    inner = jnp.logical_and(c > 0, c < NC - 1)
    pl.semaphore_wait(barrier, len(peers) + 1 + inner.astype(jnp.int32))


def remote(src, dst, send, recv, where):
    return pltpu.make_async_remote_copy(
        src_ref=src, dst_ref=dst, send_sem=send, recv_sem=recv, device_id=dev(*where), device_id_type=MESH
    )


def local(src, dst, sem):
    return pltpu.make_async_copy(src, dst, sem)


def at(rel):
    return NZ - 1 if abs(rel) == 4 else 2 * rel if rel >= 0 else -2 * rel - 1


def head_cols(x, h):
    return pl.ds(pl.multiple_of((x * HPD + h) * HDIM, HDIM), HDIM)


def nt(a, b):
    return lax.dot_general(a, b, (((1,), (1,)), ((), ())), preferred_element_type=jnp.float32)


def tn(a, b):
    return lax.dot_general(a, b, (((0,), (0,)), ((), ())), preferred_element_type=jnp.float32)


def nn(a, b):
    return lax.dot_general(a, b, (((1,), (0,)), ((), ())), preferred_element_type=jnp.float32)


def kernel(
    q, g, k, v, lists, out_q, out_k, out_v,
    kv0, kv1, kv2, qg0, qg1, qg2, dq0, dq1, dq2, part0, part1, part2, edge0, edge1, edge2,
    moving0, moving1, moving2, landed0, landed1, landed2, final0, final1, final2,
    pads, mine, lists_v, lists_s, runs, leaving, home,
    sent, up_sent, down_sent, audio_sem, video_sem, ring_sem, spread_sem, edge_sem, sum_sem, out_sem, home_sem, list_sem,
):
    c, s = lax.axis_index("grp"), lax.axis_index("seq")
    x, z = s // NZ, s % NZ
    enter(c, x, z)
    audio, video, outs = (k, v), (q, g), (out_k, out_v)
    kv, qg, dq = (kv0, kv1, kv2), (qg0, qg1, qg2), (dq0, dq1, dq2)
    part, edge = (part0, part1, part2), (edge0, edge1, edge2)
    moving, landed, final = (moving0, moving1, moving2), (landed0, landed1, landed2), (final0, final1, final2)
    above, below = jnp.minimum(c + 1, NC - 1), jnp.maximum(c - 1, 0)
    has_above, has_below = c < NC - 1, c > 0
    AUDIO, VIDEO, LIST, RING, SUM, QUERY, FINAL, HOME = (sent.at[i] for i in range(8))

    def awaited(ref, sem):
        local(ref, ref, sem).wait()

    def peers():
        return [(x + r) % NX for r in range(1, NX)]

    def along(sign, hops):
        return (c, x, (z + sign * hops + NZ) % NZ)

    def send_audio(h):
        for w in range(2):
            for to in peers():
                source, target = audio[w].at[:, head_cols(to, h)], kv[h].at[w, 2 + x, 0]
                remote(source, target, AUDIO, audio_sem.at[h], (c, to, z)).start()
            local(audio[w].at[:, head_cols(x, h)], kv[h].at[w, 2 + x, 0], audio_sem.at[h]).start()

    def send_video(h):
        for w in range(2):
            for to in peers():
                source, target = video[w].at[:, head_cols(to, h)], qg[h].at[w, x]
                remote(source, target, VIDEO, video_sem.at[h], (c, to, z)).start()
            local(video[w].at[:, head_cols(x, h)], qg[h].at[w, x], video_sem.at[h]).start()

    def onward(h, d, step, piece):
        sign = 1 - 2 * d
        what = pl.ds(*piece) if step < 3 else pl.ds(d, 1)
        source = kv[h].at[what, pl.ds(2, NX), at(-sign * step)]
        target = kv[h].at[what, pl.ds(2, NX), at(-sign * (step + 1))]
        return remote(source, target, RING, ring_sem.at[h, d, step, piece[0]], along(sign, 1))

    def spread(h, low, count):
        span = pl.ds(low, count)

        @pl.when(has_above)
        def _():
            source, target = kv[h].at[:, pl.ds(4, 2), span], kv[h].at[:, pl.ds(0, 2), span]
            remote(source, target, up_sent.at[0], spread_sem.at[h, 0], (above, x, z)).start()

        @pl.when(has_below)
        def _():
            source, target = kv[h].at[:, pl.ds(2, 2), span], kv[h].at[:, pl.ds(6, 2), span]
            remote(source, target, down_sent.at[0], spread_sem.at[h, 1], (below, x, z)).start()

    def ready(h):
        awaited(qg[h], video_sem.at[h])

        @pl.when(has_above)
        def _():
            awaited(kv[h].at[:, pl.ds(6, 2)], spread_sem.at[h, 1])

        @pl.when(has_below)
        def _():
            awaited(kv[h].at[:, pl.ds(0, 2)], spread_sem.at[h, 0])

    def there(h, step):
        if step == 0:
            awaited(kv[h].at[:, pl.ds(2, NX), 0], audio_sem.at[h])
        for piece in PIECES:
            for d in range(2):
                ends = d in range(piece[0], sum(piece))
                if step and (step < 4 or ends):
                    onward(h, d, step - 1, piece).wait_recv()
                if step < 3 or (step == 3 and ends):
                    onward(h, d, step, piece).start()
        if step > 1:
            spread(h, *SPREADS[step - 2])

    def send_lists():
        mine[...] = jnp.zeros_like(mine)
        mine[0:2, 0:LMAX] = lists[...]
        for to in peers():
            remote(mine, lists_v.at[x], LIST, list_sem.at[0], (c, to, z)).start()
        local(mine, lists_v.at[x], list_sem.at[0]).start()

    def clear():
        pads[:, :, 0:LMAX] = jnp.zeros((TILES, 2, LMAX, ROWS, HDIM), jnp.float32)
        pads[:, :, 2 * LMAX : 3 * LMAX] = jnp.zeros((TILES, 2, LMAX, ROWS, HDIM), jnp.float32)
        for h in range(HPD):

            @pl.when(c == 0)
            def _():
                edge[h][:, 0] = jnp.zeros((2,) + edge[h].shape[2:], BF16)

            @pl.when(c == NC - 1)
            def _():
                edge[h][:, 1] = jnp.zeros((2,) + edge[h].shape[2:], BF16)

    def read_lists():
        awaited(lists_v, list_sem.at[0])
        fetched = local(lists_v, lists_s, list_sem.at[1])
        fetched.start()
        fetched.wait()
        for t in range(TILES):
            count = jnp.int32(0)
            for j in range(LMAX):
                count += (lists_s[t // 2, t % 2, j] >= 0).astype(jnp.int32)
            runs[0, t] = jnp.clip(lists_s[t // 2, t % 2, 0] - (c * NX * NZ - NX * NZ // 2), 0, WIN - 1)
            runs[1, t] = count

    scale = HDIM**-0.5

    def tiles(h):
        loaded, ready_terms = [], []
        for t in range(TILES):
            first, count = runs[0, t], runs[1, t]
            blocks = [jnp.minimum(first + jnp.where(j < count, j, 0), WIN - 1) for j in range(LMAX)]
            places = [(e >> 3, ((e & 7) - z + NZ) & 7) for e in blocks]
            places = [(line, jnp.where(rel < 4, 2 * rel, 15 - 2 * rel)) for line, rel in places]
            kt = jnp.concatenate([kv[h][0, line, where] for line, where in places], axis=0)
            vt = jnp.concatenate([kv[h][1, line, where] for line, where in places], axis=0)
            rows = pl.ds(t % 2 * VBLK, VBLK)
            qt, gt = qg[h][0, t // 2, rows], qg[h][1, t // 2, rows]
            loaded.append((count, kt, qt, gt, nt(kt, qt), nt(vt, gt)))
        for count, kt, qt, gt, products, grad_weights in loaded:
            dead = [jnp.full((ROWS, VBLK), jnp.where(j < count, 0.0, MASKED), jnp.float32) for j in range(LMAX)]
            scores = products * (scale * LOG2E) + jnp.concatenate(dead, axis=0)
            raw = jnp.exp2(scores - jnp.max(scores, axis=0, keepdims=True))
            inverse = 1.0 / jnp.sum(raw, axis=0, keepdims=True)
            inner = jnp.sum(raw * grad_weights, axis=0, keepdims=True) * inverse
            weights_low = (raw * inverse).astype(BF16)
            grad_scores = (raw * ((grad_weights - inner) * (inverse * scale))).astype(BF16)
            ready_terms.append((kt, qt, gt, weights_low, grad_scores))
        for t, (kt, qt, gt, weights_low, grad_scores) in enumerate(ready_terms):
            pads[t, 1, LMAX : 2 * LMAX] = nn(weights_low, gt).reshape(LMAX, ROWS, HDIM)
            pads[t, 0, LMAX : 2 * LMAX] = nn(grad_scores, qt).reshape(LMAX, ROWS, HDIM)
            dq[h][t // 2, pl.ds(t % 2 * VBLK, VBLK)] = tn(grad_scores, kt).astype(BF16)

    def place(h):
        for w in range(2):
            for line in range(2 * NX):
                near = range(max(0, line - NX) * 2, min(NX, line + 1) * 2)
                total = None
                for t in near:
                    term = pads[t, w, pl.ds(jnp.clip(line * NZ - runs[0, t] + LMAX, 0, 2 * LMAX), LMAX)]
                    total = term if total is None else total + term
                total = total.astype(BF16)
                for zz in range(NZ):
                    rel = (zz - z + NZ) & 7
                    part[h][w, line, jnp.where(rel < 4, 2 * rel, 15 - 2 * rel)] = total[zz]

    def edge_copy(h, d, part_of):
        low, count = EDGES[part_of]
        line, to, sem = ((6, above, up_sent), (0, below, down_sent))[d]
        source, target = part[h].at[:, pl.ds(line, 2), pl.ds(low, count)], edge[h].at[:, d, :, pl.ds(low, count)]
        return remote(source, target, sem.at[1], edge_sem.at[h, d, part_of], (to, x, z))

    def send_edges(h, part_of):
        @pl.when(has_above)
        def _():
            edge_copy(h, 0, part_of).start()

        @pl.when(has_below)
        def _():
            edge_copy(h, 1, part_of).start()

    def send_queries(h):
        for to in peers():
            remote(dq[h].at[to], out_q.at[:, head_cols(x, h)], QUERY, out_sem.at[2], (c, to, z)).start()
        local(dq[h].at[x], out_q.at[:, head_cols(x, h)], out_sem.at[2]).start()

    def edges_in(h, part_of):
        @pl.when(has_above)
        def _():
            edge_copy(h, 1, part_of).wait_recv()

        @pl.when(has_below)
        def _():
            edge_copy(h, 0, part_of).wait_recv()

    def total(h, w, rel):
        p = at(rel)
        low = part[h][w, 2:4, p].astype(jnp.float32) + edge[h][w, 0, :, p].astype(jnp.float32)
        high = part[h][w, 4:6, p].astype(jnp.float32) + edge[h][w, 1, :, p].astype(jnp.float32)
        return jnp.concatenate([low, high], axis=0)

    def sum_copy(h, d, dist, piece):
        what = pl.ds(*piece) if dist < 4 else pl.ds(d, 1)
        source, target = moving[h].at[d, dist - 1, what], landed[h].at[d, dist - 1, what]
        return remote(source, target, SUM, sum_sem.at[h, d, dist - 1, piece[0]], along(1 - 2 * d, 1))

    def sums(h, dist):
        if dist > 1:
            edges_in(h, 4 - dist)
        for piece in PIECES:
            for d in range(2):
                ends = d in range(piece[0], sum(piece))
                if dist == 4 and not ends:
                    continue
                if dist < 3 or (dist == 3 and ends):
                    sum_copy(h, d, dist + 1, piece).wait_recv()
                for w in range(piece[0], sum(piece)):
                    if dist == 4 and w != d:
                        continue
                    value = total(h, w, -dist if d else dist)
                    if dist < 3 or (dist == 3 and w == d):
                        value = value + landed[h][d, dist, w].astype(jnp.float32)
                    if HOMING and h == LATE and dist == 1:
                        send_home(w, 1 - 2 * d, value)
                    else:
                        moving[h][d, dist - 1, w] = value.astype(BF16)
                if not (HOMING and h == LATE and dist == 1):
                    sum_copy(h, d, dist, piece).start()

    def finish(h):
        for piece in PIECES:
            for d in range(2):
                sum_copy(h, d, 1, piece).wait_recv()
        for w in range(2):
            value = total(h, w, 0)
            for d in range(2):
                value = value + landed[h][d, 0, w].astype(jnp.float32)
            final[h][w] = value.astype(BF16)
            target = outs[w].at[:, head_cols(x, h)]
            for to in peers():
                remote(final[h].at[w, to], target, FINAL, out_sem.at[w], (c, to, z)).start()
            local(final[h].at[w, x], target, out_sem.at[w]).start()

    def send_home(w, rel, value):
        leaving[w, at(rel)] = value.astype(BF16)
        for r in range(NX):
            to = (x + r) % NX
            source, target = leaving.at[w, at(rel), to], home.at[w, x, at(-rel)]
            if rel or r:
                remote(source, target, HOME, home_sem.at[0], (c, to, (z + rel + NZ) % NZ)).start()
            else:
                local(source, target, home_sem.at[0]).start()

    def last_finish():
        awaited(home, home_sem.at[0])
        for w in range(2):
            value = home[w, :, 0].astype(jnp.float32)
            for i in range(1, 3):
                value = value + home[w, :, i].astype(jnp.float32)
            final[LATE][w] = value.astype(BF16)
            for line in range(NX):
                local(final[LATE].at[w, line], outs[w].at[:, head_cols(line, LATE)], out_sem.at[w]).start()

    def compute(h):
        ready(h)
        tiles(h)
        place(h)
        send_edges(h, 0)
        send_edges(h, 1)
        send_queries(h)

    def back(h, dist):
        if HOMING and h == LATE and dist == 1:
            for w in range(2):
                send_home(w, 0, total(h, w, 0))
        if dist:
            sums(h, dist)
        elif HOMING and h == LATE:
            last_finish()
        else:
            finish(h)

    def edges(h):
        send_edges(h, 2)

    for action, *arguments in SCHEDULE:
        {
            "audio": send_audio, "video": send_video, "lists": send_lists, "clear": clear, "read": read_lists,
            "there": there, "compute": compute, "edges": edges, "back": back,
        }[action](*arguments)

    awaited(out_q, out_sem.at[2])
    for w in range(2):
        awaited(outs[w], out_sem.at[w])
    for i in range(2):

        @pl.when(has_above)
        def _():
            awaited(pads.at[pl.ds(0, 2), 0], up_sent.at[i])

        @pl.when(has_below)
        def _():
            awaited(pads.at[pl.ds(0, 2), 0], down_sent.at[i])

    homing = 1 if HOMING else 0
    for sem, a, b in (
        (AUDIO, 1, 9), (VIDEO, 3, 24), (RING, 4, 21), (SUM, 4, 21 - 2 * homing), (QUERY, 3, 12), (FINAL, 1, 9 - 3 * homing),
        (HOME, 1, 11 * homing),
    ):
        if b:
            awaited(pads.at[pl.ds(0, a), 0, pl.ds(0, b)], sem)
    awaited(lists_v.at[pl.ds(0, NX - 1)], LIST)


HBM = pl.BlockSpec(memory_space=pltpu.HBM)
VMEM = pl.BlockSpec(memory_space=pltpu.VMEM)


def sems(*shape):
    return pltpu.SemaphoreType.DMA(shape)


def each(*shape):
    return [pltpu.VMEM(shape, BF16)] * HPD


def per_device(q, k, v, g, lists):
    return pl.pallas_call(
        kernel,
        out_shape=tuple(jax.ShapeDtypeStruct(a.shape, BF16) for a in (q, k, v)),
        in_specs=[HBM] * 4 + [VMEM],
        out_specs=(HBM,) * 3,
        scratch_shapes=[
            *each(2, 2 * NX, NZ, ROWS, HDIM),
            *each(2, NX, VROWS, HDIM),
            *each(NX, VROWS, HDIM),
            *each(2, 2 * NX, NZ, ROWS, HDIM),
            *each(2, 2, 2, NZ, ROWS, HDIM),
            *each(2, 4, 2, NX, ROWS, HDIM),
            *each(2, 4, 2, NX, ROWS, HDIM),
            *each(2, NX, ROWS, HDIM),
            pltpu.VMEM((TILES, 2, 3 * LMAX, ROWS, HDIM), jnp.float32),
            pltpu.VMEM((8, 128), jnp.int32),
            pltpu.VMEM((NX, 8, 128), jnp.int32),
            pltpu.SMEM((NX, 8, 128), jnp.int32),
            pltpu.SMEM((2, TILES), jnp.int32),
            pltpu.VMEM((2, 3, NX, ROWS, HDIM), BF16),
            pltpu.VMEM((2, NX, 3, ROWS, HDIM), BF16),
            sems(8), sems(2), sems(2), sems(HPD), sems(HPD), sems(HPD, 2, 4, len(PIECES)), sems(HPD, 2),
            sems(HPD, 2, len(EDGES)), sems(HPD, 2, 4, len(PIECES)), sems(3), sems(1), sems(2),
        ],
        compiler_params=pltpu.CompilerParams(
            collective_id=0, has_side_effects=True, vmem_limit_bytes=62 * 2**20
        ),
        name="cross_attention_backward",
    )(q, g, k, v, lists)


def solution(mesh):
    placed = P(("grp", "seq"), None)
    return jax.shard_map(
        per_device,
        mesh=mesh,
        in_specs=(placed,) * 5,
        out_specs=(placed,) * 3,
        check_vma=False,
    )
```

```python
import jax
import jax.numpy as jnp
from jax import lax
from jax.experimental import pallas as pl
from jax.experimental.pallas import tpu as pltpu
from jax.sharding import PartitionSpec as P

MESH = pl.DeviceIdType.MESH
HEADS = 12
HDIM = 128
NX, NZ, NC = 4, 8, 8
HPD = HEADS // NX
ROWS = 32
VROWS = 256
VBLK = 128
LMAX = 8
KEYS = LMAX * ROWS
WIN = 2 * NX * NZ
TILES = 2 * NX
SPREADS = ((0, 5), (5, 2), (7, 1))
EDGES = ((7, 1), (5, 2), (0, 5))
MASKED = -1e30
LOG2E = 1.4426950408889634
BF16 = jnp.bfloat16


SCHEDULE = (
    ("audio", 0), ("audio", 1), ("audio", 2), ("lists",), ("video", 0),
    ("clear",), ("there", 0, 1), ("there", 1, 1), ("there", 2, 1),
    ("video", 1), ("there", 0, 2), ("there", 1, 2), ("there", 2, 2), ("video", 2), ("there", 0, 3), ("there", 1, 3),
    ("there", 2, 3), ("read",), ("there", 0, 4), ("there", 1, 4), ("there", 2, 4),
    ("compute", 0), ("compute", 1), ("compute", 2), ("edges", 0), ("edges", 1), ("edges", 2),
    ("back", 0, 4), ("back", 1, 4), ("back", 2, 4),
    ("back", 0, 3), ("back", 1, 3), ("back", 2, 3), ("back", 0, 2), ("back", 1, 2), ("back", 2, 2),
    ("own", 0), ("own", 1), ("own", 2), ("back", 0, 1), ("back", 1, 1), ("back", 2, 1), ("finish", 0), ("finish", 1), ("finish", 2),
)


def dev(c, x, z):
    return {"grp": c, "seq": x * NZ + z}


def enter(c, x, z):
    barrier = pltpu.get_barrier_semaphore()

    def greet(*where):
        pl.semaphore_signal(barrier, inc=1, device_id=dev(*where), device_id_type=MESH)

    peers = [(r, dz) for dz in (-1, 0, 1) for r in range(NX) if r or dz]
    for r, dz in peers:
        greet(c, (x + r) % NX, (z + dz + NZ) % NZ)

    @pl.when(c > 0)
    def _():
        greet(c - 1, x, z)

    @pl.when(c < NC - 1)
    def _():
        greet(c + 1, x, z)

    inner = jnp.logical_and(c > 0, c < NC - 1)
    pl.semaphore_wait(barrier, len(peers) + 1 + inner.astype(jnp.int32))


def remote(src, dst, send, recv, where):
    return pltpu.make_async_remote_copy(
        src_ref=src, dst_ref=dst, send_sem=send, recv_sem=recv, device_id=dev(*where), device_id_type=MESH
    )


def local(src, dst, sem):
    return pltpu.make_async_copy(src, dst, sem)


def at(rel):
    return NZ - 1 if abs(rel) == 4 else 2 * rel if rel >= 0 else -2 * rel - 1


def head_cols(x, h):
    return pl.ds(pl.multiple_of((x * HPD + h) * HDIM, HDIM), HDIM)


def nt(a, b):
    return lax.dot_general(a, b, (((1,), (1,)), ((), ())), preferred_element_type=jnp.float32)


def tn(a, b):
    return lax.dot_general(a, b, (((0,), (0,)), ((), ())), preferred_element_type=jnp.float32)


def nn(a, b):
    return lax.dot_general(a, b, (((1,), (0,)), ((), ())), preferred_element_type=jnp.float32)


def kernel(
    q, g, k, v, lists, out_q, out_k, out_v,
    kv0, kv1, kv2, qg0, qg1, qg2, dq0, dq1, dq2, part0, part1, part2, edge0, edge1, edge2,
    moving0, moving1, moving2, landed0, landed1, landed2, final0, final1, final2,
    pads, mine, lists_v, lists_s, runs, leaving, home0, home1, home2,
    sent, up_sent, down_sent, audio_sem, video_sem, ring_sem, spread_sem, edge_sem, sum_sem, out_sem, home_sem, list_sem,
):
    c, s = lax.axis_index("grp"), lax.axis_index("seq")
    x, z = s // NZ, s % NZ
    enter(c, x, z)
    audio, video, outs = (k, v), (q, g), (out_k, out_v)
    kv, qg, dq = (kv0, kv1, kv2), (qg0, qg1, qg2), (dq0, dq1, dq2)
    part, edge = (part0, part1, part2), (edge0, edge1, edge2)
    moving, landed, final = (moving0, moving1, moving2), (landed0, landed1, landed2), (final0, final1, final2)
    home = (home0, home1, home2)
    above, below = jnp.minimum(c + 1, NC - 1), jnp.maximum(c - 1, 0)
    has_above, has_below = c < NC - 1, c > 0
    AUDIO, VIDEO, LIST, RING, SUM, QUERY, HOME = (sent.at[i] for i in range(7))

    def awaited(ref, sem):
        local(ref, ref, sem).wait()

    def peers():
        return [(x + r) % NX for r in range(1, NX)]

    def along(sign, hops):
        return (c, x, (z + sign * hops + NZ) % NZ)

    def send_audio(h):
        for w in range(2):
            for dz in (1, -1, 0):
                for r in range(NX):
                    to = (x + r) % NX
                    source, target = audio[w].at[:, head_cols(to, h)], kv[h].at[w, 2 + x, at(-dz)]
                    if dz or r:
                        remote(source, target, AUDIO, audio_sem.at[h, at(dz)], (c, to, (z + dz + NZ) % NZ)).start()
                    else:
                        local(source, target, audio_sem.at[h, 0]).start()

    def audio_in(h, dz):
        awaited(kv[h].at[:, pl.ds(2, NX), at(-dz)], audio_sem.at[h, at(dz)])

    def send_video(h):
        for w in range(2):
            for to in peers():
                source, target = video[w].at[:, head_cols(to, h)], qg[h].at[w, x]
                remote(source, target, VIDEO, video_sem.at[h], (c, to, z)).start()
            local(video[w].at[:, head_cols(x, h)], qg[h].at[w, x], video_sem.at[h]).start()

    def onward(h, d, step):
        sign = 1 - 2 * d
        what = pl.ds(0, 2) if step < 3 else pl.ds(d, 1)
        source = kv[h].at[what, pl.ds(2, NX), at(-sign * step)]
        target = kv[h].at[what, pl.ds(2, NX), at(-sign * (step + 1))]
        return remote(source, target, RING, ring_sem.at[h, d, step - 1], along(sign, 1))

    def spread(h, low, count):
        span = pl.ds(low, count)

        @pl.when(has_above)
        def _():
            source, target = kv[h].at[:, pl.ds(4, 2), span], kv[h].at[:, pl.ds(0, 2), span]
            remote(source, target, up_sent.at[0], spread_sem.at[h, 0], (above, x, z)).start()

        @pl.when(has_below)
        def _():
            source, target = kv[h].at[:, pl.ds(2, 2), span], kv[h].at[:, pl.ds(6, 2), span]
            remote(source, target, down_sent.at[0], spread_sem.at[h, 1], (below, x, z)).start()

    def ready(h):
        awaited(qg[h], video_sem.at[h])

        @pl.when(has_above)
        def _():
            awaited(kv[h].at[:, pl.ds(6, 2)], spread_sem.at[h, 1])

        @pl.when(has_below)
        def _():
            awaited(kv[h].at[:, pl.ds(0, 2)], spread_sem.at[h, 0])

    def there(h, step):
        for d in range(2):
            if step == 1:
                audio_in(h, 1 - 2 * d)
            else:
                onward(h, d, step - 1).wait_recv()
            if step < 4:
                onward(h, d, step).start()
        if step == 2:
            audio_in(h, 0)
        if step > 1:
            spread(h, *SPREADS[step - 2])

    def send_lists():
        mine[...] = jnp.zeros_like(mine)
        mine[0:2, 0:LMAX] = lists[...]
        for to in peers():
            remote(mine, lists_v.at[x], LIST, list_sem.at[0], (c, to, z)).start()
        local(mine, lists_v.at[x], list_sem.at[0]).start()

    def clear():
        pads[:, :, 0:LMAX] = jnp.zeros((TILES, 2, LMAX, ROWS, HDIM), jnp.float32)
        pads[:, :, 2 * LMAX : 3 * LMAX] = jnp.zeros((TILES, 2, LMAX, ROWS, HDIM), jnp.float32)
        for h in range(HPD):

            @pl.when(c == 0)
            def _():
                edge[h][:, 0] = jnp.zeros((2,) + edge[h].shape[2:], BF16)

            @pl.when(c == NC - 1)
            def _():
                edge[h][:, 1] = jnp.zeros((2,) + edge[h].shape[2:], BF16)

    def read_lists():
        awaited(lists_v, list_sem.at[0])
        fetched = local(lists_v, lists_s, list_sem.at[1])
        fetched.start()
        fetched.wait()
        for t in range(TILES):
            count = jnp.int32(0)
            for j in range(LMAX):
                count += (lists_s[t // 2, t % 2, j] >= 0).astype(jnp.int32)
            runs[0, t] = jnp.clip(lists_s[t // 2, t % 2, 0] - (c * NX * NZ - NX * NZ // 2), 0, WIN - 1)
            runs[1, t] = count

    scale = HDIM**-0.5

    def tiles(h):
        loaded, ready_terms = [], []
        for t in range(TILES):
            first, count = runs[0, t], runs[1, t]
            blocks = [jnp.minimum(first + jnp.where(j < count, j, 0), WIN - 1) for j in range(LMAX)]
            places = [(e >> 3, ((e & 7) - z + NZ) & 7) for e in blocks]
            places = [(line, jnp.where(rel < 4, 2 * rel, 15 - 2 * rel)) for line, rel in places]
            kt = jnp.concatenate([kv[h][0, line, where] for line, where in places], axis=0)
            vt = jnp.concatenate([kv[h][1, line, where] for line, where in places], axis=0)
            rows = pl.ds(t % 2 * VBLK, VBLK)
            qt, gt = qg[h][0, t // 2, rows], qg[h][1, t // 2, rows]
            loaded.append((count, kt, qt, gt, nt(kt, qt), nt(vt, gt)))
        for count, kt, qt, gt, products, grad_weights in loaded:
            dead = [jnp.full((ROWS, VBLK), jnp.where(j < count, 0.0, MASKED), jnp.float32) for j in range(LMAX)]
            scores = products * (scale * LOG2E) + jnp.concatenate(dead, axis=0)
            raw = jnp.exp2(scores - jnp.max(scores, axis=0, keepdims=True))
            inverse = 1.0 / jnp.sum(raw, axis=0, keepdims=True)
            inner = jnp.sum(raw * grad_weights, axis=0, keepdims=True) * inverse
            weights_low = (raw * inverse).astype(BF16)
            grad_scores = (raw * ((grad_weights - inner) * (inverse * scale))).astype(BF16)
            ready_terms.append((kt, qt, gt, weights_low, grad_scores))
        for t, (kt, qt, gt, weights_low, grad_scores) in enumerate(ready_terms):
            pads[t, 1, LMAX : 2 * LMAX] = nn(weights_low, gt).reshape(LMAX, ROWS, HDIM)
            pads[t, 0, LMAX : 2 * LMAX] = nn(grad_scores, qt).reshape(LMAX, ROWS, HDIM)
            dq[h][t // 2, pl.ds(t % 2 * VBLK, VBLK)] = tn(grad_scores, kt).astype(BF16)

    def place(h):
        for w in range(2):
            for line in range(2 * NX):
                near = range(max(0, line - NX) * 2, min(NX, line + 1) * 2)
                total = None
                for t in near:
                    term = pads[t, w, pl.ds(jnp.clip(line * NZ - runs[0, t] + LMAX, 0, 2 * LMAX), LMAX)]
                    total = term if total is None else total + term
                total = total.astype(BF16)
                for zz in range(NZ):
                    rel = (zz - z + NZ) & 7
                    part[h][w, line, jnp.where(rel < 4, 2 * rel, 15 - 2 * rel)] = total[zz]

    def edge_copy(h, d, part_of):
        low, count = EDGES[part_of]
        line, to, sem = ((6, above, up_sent), (0, below, down_sent))[d]
        source, target = part[h].at[:, pl.ds(line, 2), pl.ds(low, count)], edge[h].at[:, d, :, pl.ds(low, count)]
        return remote(source, target, sem.at[1], edge_sem.at[h, d, part_of], (to, x, z))

    def send_edges(h, part_of):
        @pl.when(has_above)
        def _():
            edge_copy(h, 0, part_of).start()

        @pl.when(has_below)
        def _():
            edge_copy(h, 1, part_of).start()

    def send_queries(h):
        for to in peers():
            remote(dq[h].at[to], out_q.at[:, head_cols(x, h)], QUERY, out_sem.at[2], (c, to, z)).start()
        local(dq[h].at[x], out_q.at[:, head_cols(x, h)], out_sem.at[2]).start()

    def edges_in(h, part_of):
        @pl.when(has_above)
        def _():
            edge_copy(h, 1, part_of).wait_recv()

        @pl.when(has_below)
        def _():
            edge_copy(h, 0, part_of).wait_recv()

    def total(h, w, rel):
        p = at(rel)
        low = part[h][w, 2:4, p].astype(jnp.float32) + edge[h][w, 0, :, p].astype(jnp.float32)
        high = part[h][w, 4:6, p].astype(jnp.float32) + edge[h][w, 1, :, p].astype(jnp.float32)
        return jnp.concatenate([low, high], axis=0)

    def sum_copy(h, d, dist):
        what = pl.ds(0, 2) if dist < 4 else pl.ds(d, 1)
        source, target = moving[h].at[d, dist - 2, what], landed[h].at[d, dist - 2, what]
        return remote(source, target, SUM, sum_sem.at[h, d, dist - 2], along(1 - 2 * d, 1))

    def send_home(h, w, rel, value):
        leaving[h, w, at(rel)] = value.astype(BF16)
        for r in range(NX):
            to = (x + r) % NX
            source, target = leaving.at[h, w, at(rel), to], home[h].at[w, x, at(-rel)]
            if rel or r:
                remote(source, target, HOME, home_sem.at[h], (c, to, (z + rel + NZ) % NZ)).start()
            else:
                local(source, target, home_sem.at[h]).start()

    def back(h, dist):
        if dist > 1:
            edges_in(h, 4 - dist)
        for d in range(2):
            if dist < 4:
                sum_copy(h, d, dist + 1).wait_recv()
            for w in range(2):
                if dist == 4 and w != d:
                    continue
                value = total(h, w, -dist if d else dist)
                if dist < 3 or (dist == 3 and w == d):
                    value = value + landed[h][d, dist - 1, w].astype(jnp.float32)
                if dist == 1:
                    send_home(h, w, 1 - 2 * d, value)
                else:
                    moving[h][d, dist - 2, w] = value.astype(BF16)
            if dist > 1:
                sum_copy(h, d, dist).start()

    def own(h):
        for w in range(2):
            send_home(h, w, 0, total(h, w, 0))

    def finish(h):
        awaited(home[h], home_sem.at[h])
        for w in range(2):
            value = home[h][w, :, 0].astype(jnp.float32)
            for i in range(1, 3):
                value = value + home[h][w, :, i].astype(jnp.float32)
            final[h][w] = value.astype(BF16)
            for line in range(NX):
                local(final[h].at[w, line], outs[w].at[:, head_cols(line, h)], out_sem.at[w]).start()

    def compute(h):
        ready(h)
        tiles(h)
        place(h)
        send_edges(h, 0)
        send_edges(h, 1)
        send_queries(h)

    def edges(h):
        send_edges(h, 2)

    for action, *arguments in SCHEDULE:
        {
            "audio": send_audio, "video": send_video, "lists": send_lists, "clear": clear, "read": read_lists,
            "there": there, "compute": compute, "edges": edges, "back": back, "own": own, "finish": finish,
        }[action](*arguments)

    awaited(out_q, out_sem.at[2])
    for w in range(2):
        awaited(outs[w], out_sem.at[w])
    for i in range(2):

        @pl.when(has_above)
        def _():
            awaited(pads.at[pl.ds(0, 2), 0], up_sent.at[i])

        @pl.when(has_below)
        def _():
            awaited(pads.at[pl.ds(0, 2), 0], down_sent.at[i])

    for sem, a, b in ((AUDIO, 3, 11), (VIDEO, 3, 24), (RING, 3, 20), (SUM, 3, 20), (QUERY, 3, 12), (HOME, 3, 11)):
        awaited(pads.at[pl.ds(0, a), 0, pl.ds(0, b)], sem)
    awaited(lists_v.at[pl.ds(0, NX - 1)], LIST)


def copy_kernel(q, k, v, out_q, out_k, out_v, held_q, held_k, held_v, sem):
    half = VROWS // 2
    low, high = pl.ds(0, half), pl.ds(half, half)
    ways = (
        (q.at[low], held_q.at[low], out_q.at[low]), (q.at[high], held_q.at[high], out_q.at[high]),
        (k, held_k, out_k), (v, held_v, out_v),
    )
    first = [local(a, b, sem.at[0, i]) for i, (a, b, _) in enumerate(ways)]
    second = [local(b, o, sem.at[1, i]) for i, (_, b, o) in enumerate(ways)]
    for copy in first:
        copy.start()
    for one, two in zip(first, second):
        one.wait()
        two.start()
    for copy in second:
        copy.wait()


HBM = pl.BlockSpec(memory_space=pltpu.HBM)
VMEM = pl.BlockSpec(memory_space=pltpu.VMEM)


def sems(*shape):
    return pltpu.SemaphoreType.DMA(shape)


def each(*shape):
    return [pltpu.VMEM(shape, BF16)] * HPD


def per_device(q, k, v, g, lists):
    grads = pl.pallas_call(
        kernel,
        out_shape=tuple(jax.ShapeDtypeStruct(a.shape, BF16) for a in (q, k, v)),
        in_specs=[HBM] * 4 + [VMEM],
        out_specs=(HBM,) * 3,
        scratch_shapes=[
            *each(2, 2 * NX, NZ, ROWS, HDIM),
            *each(2, NX, VROWS, HDIM),
            *each(NX, VROWS, HDIM),
            *each(2, 2 * NX, NZ, ROWS, HDIM),
            *each(2, 2, 2, NZ, ROWS, HDIM),
            *each(2, 3, 2, NX, ROWS, HDIM),
            *each(2, 3, 2, NX, ROWS, HDIM),
            *each(2, NX, ROWS, HDIM),
            pltpu.VMEM((TILES, 2, 3 * LMAX, ROWS, HDIM), jnp.float32),
            pltpu.VMEM((8, 128), jnp.int32),
            pltpu.VMEM((NX, 8, 128), jnp.int32),
            pltpu.SMEM((NX, 8, 128), jnp.int32),
            pltpu.SMEM((2, TILES), jnp.int32),
            pltpu.VMEM((HPD, 2, 3, NX, ROWS, HDIM), BF16),
            *each(2, NX, 3, ROWS, HDIM),
            sems(7), sems(2), sems(2), sems(HPD, 3), sems(HPD), sems(HPD, 2, 3), sems(HPD, 2),
            sems(HPD, 2, len(EDGES)), sems(HPD, 2, 3), sems(3), sems(HPD), sems(2),
        ],
        compiler_params=pltpu.CompilerParams(
            collective_id=0, has_side_effects=True, vmem_limit_bytes=62 * 2**20
        ),
        name="cross_attention_backward",
    )(q, g, k, v, lists)
    return pl.pallas_call(
        copy_kernel,
        out_shape=tuple(jax.ShapeDtypeStruct(a.shape, BF16) for a in (q, k, v)),
        in_specs=[HBM] * 3,
        out_specs=(HBM,) * 3,
        scratch_shapes=[*(pltpu.VMEM(a.shape, BF16) for a in (q, k, v)), sems(2, 4)],
        name="final_copies",
    )(*grads)


def solution(mesh):
    placed = P(("grp", "seq"), None)
    return jax.shard_map(
        per_device,
        mesh=mesh,
        in_specs=(placed,) * 5,
        out_specs=(placed,) * 3,
        check_vma=False,
    )
```

```python
import jax
import jax.numpy as jnp
from jax import lax
from jax.experimental import pallas as pl
from jax.experimental.pallas import tpu as pltpu
from jax.sharding import PartitionSpec as P

MESH = pl.DeviceIdType.MESH
HEADS = 12
HDIM = 128
NX, NZ, NC = 4, 8, 8
HPD = HEADS // NX
ROWS = 32
VROWS = 256
VBLK = 128
LMAX = 8
KEYS = LMAX * ROWS
WIN = 2 * NX * NZ
TILES = 2 * NX
NEAR = 1
SPREADS = ((0, 5), (5, 2), (7, 1))
EDGES = ((7, 1), (5, 2), (0, 5))
MASKED = -1e30
LOG2E = 1.4426950408889634
BF16 = jnp.bfloat16


SCHEDULE = (
    ("audio", 0), ("audio", 1), ("audio", 2), ("there", 1, 0), ("there", 2, 0), ("lists",), ("video", 0),
    ("clear",), ("there", 0, 1), ("there", 1, 1), ("there", 2, 1),
    ("video", 1), ("there", 0, 2), ("there", 1, 2), ("there", 2, 2), ("video", 2), ("there", 0, 3), ("there", 1, 3),
    ("there", 2, 3), ("read",), ("there", 0, 4), ("there", 1, 4), ("there", 2, 4),
    ("compute", 0), ("compute", 1), ("compute", 2), ("edges", 0), ("edges", 1), ("edges", 2),
    ("back", 0, 4), ("back", 1, 4), ("back", 2, 4),
    ("back", 0, 3), ("back", 1, 3), ("back", 2, 3), ("back", 0, 2), ("back", 1, 2), ("back", 2, 2),
    ("own", 0), ("own", 1), ("own", 2), ("back", 0, 1), ("back", 1, 1), ("back", 2, 1), ("finish", 0), ("finish", 1), ("finish", 2),
)


def dev(c, x, z):
    return {"grp": c, "seq": x * NZ + z}


def enter(c, x, z):
    barrier = pltpu.get_barrier_semaphore()

    def greet(*where):
        pl.semaphore_signal(barrier, inc=1, device_id=dev(*where), device_id_type=MESH)

    peers = [(r, dz) for dz in (-1, 0, 1) for r in range(NX) if r or dz]
    for r, dz in peers:
        greet(c, (x + r) % NX, (z + dz + NZ) % NZ)

    @pl.when(c > 0)
    def _():
        greet(c - 1, x, z)

    @pl.when(c < NC - 1)
    def _():
        greet(c + 1, x, z)

    inner = jnp.logical_and(c > 0, c < NC - 1)
    pl.semaphore_wait(barrier, len(peers) + 1 + inner.astype(jnp.int32))


def remote(src, dst, send, recv, where):
    return pltpu.make_async_remote_copy(
        src_ref=src, dst_ref=dst, send_sem=send, recv_sem=recv, device_id=dev(*where), device_id_type=MESH
    )


def local(src, dst, sem):
    return pltpu.make_async_copy(src, dst, sem)


def at(rel):
    return NZ - 1 if abs(rel) == 4 else 2 * rel if rel >= 0 else -2 * rel - 1


def head_cols(x, h):
    return pl.ds(pl.multiple_of((x * HPD + h) * HDIM, HDIM), HDIM)


def nt(a, b):
    return lax.dot_general(a, b, (((1,), (1,)), ((), ())), preferred_element_type=jnp.float32)


def tn(a, b):
    return lax.dot_general(a, b, (((0,), (0,)), ((), ())), preferred_element_type=jnp.float32)


def nn(a, b):
    return lax.dot_general(a, b, (((1,), (0,)), ((), ())), preferred_element_type=jnp.float32)


def kernel(
    q, g, k, v, lists, out_q, out_k, out_v,
    kv0, kv1, kv2, qg0, qg1, qg2, dq0, dq1, dq2, part0, part1, part2, edge0, edge1, edge2,
    moving0, moving1, moving2, landed0, landed1, landed2, final0, final1, final2,
    pads, mine, lists_v, lists_s, runs, leaving, home0, home1, home2,
    sent, up_sent, down_sent, audio_sem, video_sem, ring_sem, spread_sem, edge_sem, sum_sem, out_sem, home_sem, list_sem,
):
    c, s = lax.axis_index("grp"), lax.axis_index("seq")
    x, z = s // NZ, s % NZ
    enter(c, x, z)
    audio, video, outs = (k, v), (q, g), (out_k, out_v)
    kv, qg, dq = (kv0, kv1, kv2), (qg0, qg1, qg2), (dq0, dq1, dq2)
    part, edge = (part0, part1, part2), (edge0, edge1, edge2)
    moving, landed, final = (moving0, moving1, moving2), (landed0, landed1, landed2), (final0, final1, final2)
    home = (home0, home1, home2)
    above, below = jnp.minimum(c + 1, NC - 1), jnp.maximum(c - 1, 0)
    has_above, has_below = c < NC - 1, c > 0
    AUDIO, VIDEO, LIST, RING, SUM, QUERY, HOME = (sent.at[i] for i in range(7))

    def awaited(ref, sem):
        local(ref, ref, sem).wait()

    def peers():
        return [(x + r) % NX for r in range(1, NX)]

    def along(sign, hops):
        return (c, x, (z + sign * hops + NZ) % NZ)

    def send_audio(h):
        for w in range(2):
            for dz in (1, -1, 0) if h < NEAR else (0,):
                for r in range(NX):
                    to = (x + r) % NX
                    source, target = audio[w].at[:, head_cols(to, h)], kv[h].at[w, 2 + x, at(-dz)]
                    if dz or r:
                        remote(source, target, AUDIO, audio_sem.at[h, at(dz)], (c, to, (z + dz + NZ) % NZ)).start()
                    else:
                        local(source, target, audio_sem.at[h, 0]).start()

    def audio_in(h, dz):
        awaited(kv[h].at[:, pl.ds(2, NX), at(-dz)], audio_sem.at[h, at(dz)])

    def send_video(h):
        for w in range(2):
            for to in peers():
                source, target = video[w].at[:, head_cols(to, h)], qg[h].at[w, x]
                remote(source, target, VIDEO, video_sem.at[h], (c, to, z)).start()
            local(video[w].at[:, head_cols(x, h)], qg[h].at[w, x], video_sem.at[h]).start()

    def onward(h, d, step):
        sign = 1 - 2 * d
        what = pl.ds(0, 2) if step < 3 else pl.ds(d, 1)
        source = kv[h].at[what, pl.ds(2, NX), at(-sign * step)]
        target = kv[h].at[what, pl.ds(2, NX), at(-sign * (step + 1))]
        return remote(source, target, RING, ring_sem.at[h, d, step], along(sign, 1))

    def spread(h, low, count):
        span = pl.ds(low, count)

        @pl.when(has_above)
        def _():
            source, target = kv[h].at[:, pl.ds(4, 2), span], kv[h].at[:, pl.ds(0, 2), span]
            remote(source, target, up_sent.at[0], spread_sem.at[h, 0], (above, x, z)).start()

        @pl.when(has_below)
        def _():
            source, target = kv[h].at[:, pl.ds(2, 2), span], kv[h].at[:, pl.ds(6, 2), span]
            remote(source, target, down_sent.at[0], spread_sem.at[h, 1], (below, x, z)).start()

    def ready(h):
        awaited(qg[h], video_sem.at[h])

        @pl.when(has_above)
        def _():
            awaited(kv[h].at[:, pl.ds(6, 2)], spread_sem.at[h, 1])

        @pl.when(has_below)
        def _():
            awaited(kv[h].at[:, pl.ds(0, 2)], spread_sem.at[h, 0])

    def there(h, step):
        if step == 0:
            audio_in(h, 0)
        for d in range(2):
            if step == 0:
                onward(h, d, 0).start()
                continue
            if step == 1 and h < NEAR:
                audio_in(h, 1 - 2 * d)
            else:
                onward(h, d, step - 1).wait_recv()
            if step < 4:
                onward(h, d, step).start()
        if step == 2 and h < NEAR:
            audio_in(h, 0)
        if step > 1:
            spread(h, *SPREADS[step - 2])

    def send_lists():
        mine[...] = jnp.zeros_like(mine)
        mine[0:2, 0:LMAX] = lists[...]
        for to in peers():
            remote(mine, lists_v.at[x], LIST, list_sem.at[0], (c, to, z)).start()
        local(mine, lists_v.at[x], list_sem.at[0]).start()

    def clear():
        pads[:, :, 0:LMAX] = jnp.zeros((TILES, 2, LMAX, ROWS, HDIM), jnp.float32)
        pads[:, :, 2 * LMAX : 3 * LMAX] = jnp.zeros((TILES, 2, LMAX, ROWS, HDIM), jnp.float32)
        for h in range(HPD):

            @pl.when(c == 0)
            def _():
                edge[h][:, 0] = jnp.zeros((2,) + edge[h].shape[2:], BF16)

            @pl.when(c == NC - 1)
            def _():
                edge[h][:, 1] = jnp.zeros((2,) + edge[h].shape[2:], BF16)

    def read_lists():
        awaited(lists_v, list_sem.at[0])
        fetched = local(lists_v, lists_s, list_sem.at[1])
        fetched.start()
        fetched.wait()
        for t in range(TILES):
            count = jnp.int32(0)
            for j in range(LMAX):
                count += (lists_s[t // 2, t % 2, j] >= 0).astype(jnp.int32)
            runs[0, t] = jnp.clip(lists_s[t // 2, t % 2, 0] - (c * NX * NZ - NX * NZ // 2), 0, WIN - 1)
            runs[1, t] = count

    scale = HDIM**-0.5

    def tiles(h):
        loaded, ready_terms = [], []
        for t in range(TILES):
            first, count = runs[0, t], runs[1, t]
            blocks = [jnp.minimum(first + jnp.where(j < count, j, 0), WIN - 1) for j in range(LMAX)]
            places = [(e >> 3, ((e & 7) - z + NZ) & 7) for e in blocks]
            places = [(line, jnp.where(rel < 4, 2 * rel, 15 - 2 * rel)) for line, rel in places]
            kt = jnp.concatenate([kv[h][0, line, where] for line, where in places], axis=0)
            vt = jnp.concatenate([kv[h][1, line, where] for line, where in places], axis=0)
            rows = pl.ds(t % 2 * VBLK, VBLK)
            qt, gt = qg[h][0, t // 2, rows], qg[h][1, t // 2, rows]
            loaded.append((count, kt, qt, gt, nt(kt, qt), nt(vt, gt)))
        for count, kt, qt, gt, products, grad_weights in loaded:
            dead = [jnp.full((ROWS, VBLK), jnp.where(j < count, 0.0, MASKED), jnp.float32) for j in range(LMAX)]
            scores = products * (scale * LOG2E) + jnp.concatenate(dead, axis=0)
            raw = jnp.exp2(scores - jnp.max(scores, axis=0, keepdims=True))
            inverse = 1.0 / jnp.sum(raw, axis=0, keepdims=True)
            inner = jnp.sum(raw * grad_weights, axis=0, keepdims=True) * inverse
            weights_low = (raw * inverse).astype(BF16)
            grad_scores = (raw * ((grad_weights - inner) * (inverse * scale))).astype(BF16)
            ready_terms.append((kt, qt, gt, weights_low, grad_scores))
        for t, (kt, qt, gt, weights_low, grad_scores) in enumerate(ready_terms):
            pads[t, 1, LMAX : 2 * LMAX] = nn(weights_low, gt).reshape(LMAX, ROWS, HDIM)
            pads[t, 0, LMAX : 2 * LMAX] = nn(grad_scores, qt).reshape(LMAX, ROWS, HDIM)
            dq[h][t // 2, pl.ds(t % 2 * VBLK, VBLK)] = tn(grad_scores, kt).astype(BF16)

    def place(h):
        for w in range(2):
            for line in range(2 * NX):
                near = range(max(0, line - NX) * 2, min(NX, line + 1) * 2)
                total = None
                for t in near:
                    term = pads[t, w, pl.ds(jnp.clip(line * NZ - runs[0, t] + LMAX, 0, 2 * LMAX), LMAX)]
                    total = term if total is None else total + term
                total = total.astype(BF16)
                for zz in range(NZ):
                    rel = (zz - z + NZ) & 7
                    part[h][w, line, jnp.where(rel < 4, 2 * rel, 15 - 2 * rel)] = total[zz]

    def edge_copy(h, d, part_of):
        low, count = EDGES[part_of]
        line, to, sem = ((6, above, up_sent), (0, below, down_sent))[d]
        source, target = part[h].at[:, pl.ds(line, 2), pl.ds(low, count)], edge[h].at[:, d, :, pl.ds(low, count)]
        return remote(source, target, sem.at[1], edge_sem.at[h, d, part_of], (to, x, z))

    def send_edges(h, part_of):
        @pl.when(has_above)
        def _():
            edge_copy(h, 0, part_of).start()

        @pl.when(has_below)
        def _():
            edge_copy(h, 1, part_of).start()

    def send_queries(h):
        for to in peers():
            remote(dq[h].at[to], out_q.at[:, head_cols(x, h)], QUERY, out_sem.at[2], (c, to, z)).start()
        local(dq[h].at[x], out_q.at[:, head_cols(x, h)], out_sem.at[2]).start()

    def edges_in(h, part_of):
        @pl.when(has_above)
        def _():
            edge_copy(h, 1, part_of).wait_recv()

        @pl.when(has_below)
        def _():
            edge_copy(h, 0, part_of).wait_recv()

    def total(h, w, rel):
        p = at(rel)
        low = part[h][w, 2:4, p].astype(jnp.float32) + edge[h][w, 0, :, p].astype(jnp.float32)
        high = part[h][w, 4:6, p].astype(jnp.float32) + edge[h][w, 1, :, p].astype(jnp.float32)
        return jnp.concatenate([low, high], axis=0)

    def sum_copy(h, d, dist):
        what = pl.ds(0, 2) if dist < 4 else pl.ds(d, 1)
        source, target = moving[h].at[d, dist - 2, what], landed[h].at[d, dist - 2, what]
        return remote(source, target, SUM, sum_sem.at[h, d, dist - 2], along(1 - 2 * d, 1))

    def send_home(h, w, rel, value):
        leaving[h, w, at(rel)] = value.astype(BF16)
        for r in range(NX):
            to = (x + r) % NX
            source, target = leaving.at[h, w, at(rel), to], home[h].at[w, x, at(-rel)]
            if rel or r:
                remote(source, target, HOME, home_sem.at[h], (c, to, (z + rel + NZ) % NZ)).start()
            else:
                local(source, target, home_sem.at[h]).start()

    def back(h, dist):
        if dist > 1:
            edges_in(h, 4 - dist)
        for d in range(2):
            if dist < 4:
                sum_copy(h, d, dist + 1).wait_recv()
            for w in range(2):
                if dist == 4 and w != d:
                    continue
                value = total(h, w, -dist if d else dist)
                if dist < 3 or (dist == 3 and w == d):
                    value = value + landed[h][d, dist - 1, w].astype(jnp.float32)
                if dist == 1:
                    send_home(h, w, 1 - 2 * d, value)
                else:
                    moving[h][d, dist - 2, w] = value.astype(BF16)
            if dist > 1:
                sum_copy(h, d, dist).start()

    def own(h):
        for w in range(2):
            send_home(h, w, 0, total(h, w, 0))

    def finish(h):
        awaited(home[h], home_sem.at[h])
        for w in range(2):
            value = home[h][w, :, 0].astype(jnp.float32)
            for i in range(1, 3):
                value = value + home[h][w, :, i].astype(jnp.float32)
            final[h][w] = value.astype(BF16)
            for line in range(NX):
                local(final[h].at[w, line], outs[w].at[:, head_cols(line, h)], out_sem.at[w]).start()

    def compute(h):
        ready(h)
        tiles(h)
        place(h)
        send_edges(h, 0)
        send_edges(h, 1)
        send_queries(h)

    def edges(h):
        send_edges(h, 2)

    for action, *arguments in SCHEDULE:
        {
            "audio": send_audio, "video": send_video, "lists": send_lists, "clear": clear, "read": read_lists,
            "there": there, "compute": compute, "edges": edges, "back": back, "own": own, "finish": finish,
        }[action](*arguments)

    awaited(out_q, out_sem.at[2])
    for w in range(2):
        awaited(outs[w], out_sem.at[w])
    for i in range(2):

        @pl.when(has_above)
        def _():
            awaited(pads.at[pl.ds(0, 2), 0], up_sent.at[i])

        @pl.when(has_below)
        def _():
            awaited(pads.at[pl.ds(0, 2), 0], down_sent.at[i])

    for sem, a, b in ((AUDIO, 1, 17), (VIDEO, 3, 24), (RING, 4, 19), (SUM, 3, 20), (QUERY, 3, 12), (HOME, 3, 11)):
        awaited(pads.at[pl.ds(0, a), 0, pl.ds(0, b)], sem)
    awaited(lists_v.at[pl.ds(0, NX - 1)], LIST)


def copy_kernel(q, k, v, out_q, out_k, out_v, held_q, held_k, held_v, sem):
    half = VROWS // 2
    low, high = pl.ds(0, half), pl.ds(half, half)
    ways = (
        (q.at[low], held_q.at[low], out_q.at[low]), (q.at[high], held_q.at[high], out_q.at[high]),
        (k, held_k, out_k), (v, held_v, out_v),
    )
    first = [local(a, b, sem.at[0, i]) for i, (a, b, _) in enumerate(ways)]
    second = [local(b, o, sem.at[1, i]) for i, (_, b, o) in enumerate(ways)]
    for copy in first:
        copy.start()
    for one, two in zip(first, second):
        one.wait()
        two.start()
    for copy in second:
        copy.wait()


HBM = pl.BlockSpec(memory_space=pltpu.HBM)
VMEM = pl.BlockSpec(memory_space=pltpu.VMEM)


def sems(*shape):
    return pltpu.SemaphoreType.DMA(shape)


def each(*shape):
    return [pltpu.VMEM(shape, BF16)] * HPD


def per_device(q, k, v, g, lists):
    grads = pl.pallas_call(
        kernel,
        out_shape=tuple(jax.ShapeDtypeStruct(a.shape, BF16) for a in (q, k, v)),
        in_specs=[HBM] * 4 + [VMEM],
        out_specs=(HBM,) * 3,
        scratch_shapes=[
            *each(2, 2 * NX, NZ, ROWS, HDIM),
            *each(2, NX, VROWS, HDIM),
            *each(NX, VROWS, HDIM),
            *each(2, 2 * NX, NZ, ROWS, HDIM),
            *each(2, 2, 2, NZ, ROWS, HDIM),
            *each(2, 3, 2, NX, ROWS, HDIM),
            *each(2, 3, 2, NX, ROWS, HDIM),
            *each(2, NX, ROWS, HDIM),
            pltpu.VMEM((TILES, 2, 3 * LMAX, ROWS, HDIM), jnp.float32),
            pltpu.VMEM((8, 128), jnp.int32),
            pltpu.VMEM((NX, 8, 128), jnp.int32),
            pltpu.SMEM((NX, 8, 128), jnp.int32),
            pltpu.SMEM((2, TILES), jnp.int32),
            pltpu.VMEM((HPD, 2, 3, NX, ROWS, HDIM), BF16),
            *each(2, NX, 3, ROWS, HDIM),
            sems(7), sems(2), sems(2), sems(HPD, 3), sems(HPD), sems(HPD, 2, 4), sems(HPD, 2),
            sems(HPD, 2, len(EDGES)), sems(HPD, 2, 3), sems(3), sems(HPD), sems(2),
        ],
        compiler_params=pltpu.CompilerParams(
            collective_id=0, has_side_effects=True, vmem_limit_bytes=62 * 2**20
        ),
        name="cross_attention_backward",
    )(q, g, k, v, lists)
    return pl.pallas_call(
        copy_kernel,
        out_shape=tuple(jax.ShapeDtypeStruct(a.shape, BF16) for a in (q, k, v)),
        in_specs=[HBM] * 3,
        out_specs=(HBM,) * 3,
        scratch_shapes=[*(pltpu.VMEM(a.shape, BF16) for a in (q, k, v)), sems(2, 4)],
        name="final_copies",
    )(*grads)


def solution(mesh):
    placed = P(("grp", "seq"), None)
    return jax.shard_map(
        per_device,
        mesh=mesh,
        in_specs=(placed,) * 5,
        out_specs=(placed,) * 3,
        check_vma=False,
    )
```

```python
import jax
import jax.numpy as jnp
from jax import lax
from jax.experimental import pallas as pl
from jax.experimental.pallas import tpu as pltpu
from jax.sharding import PartitionSpec as P

MESH = pl.DeviceIdType.MESH
HEADS = 12
HDIM = 128
NX, NZ, NC = 4, 8, 8
HPD = HEADS // NX
ROWS = 32
VROWS = 256
VBLK = 128
LMAX = 8
KEYS = LMAX * ROWS
WIN = 2 * NX * NZ
TILES = 2 * NX
NEAR = 1
SPREADS = ((0, 5), (5, 2), (7, 1))
EDGES = ((7, 1), (5, 2), (0, 5))
MASKED = -1e30
LOG2E = 1.4426950408889634
BF16 = jnp.bfloat16


SCHEDULE = (
    ("audio", 0), ("audio", 1), ("audio", 2), ("there", 1, 0), ("there", 2, 0), ("lists",), ("video", 0),
    ("there", 0, 1), ("there", 1, 1), ("there", 2, 1), ("clear",),
    ("video", 1), ("there", 0, 2), ("there", 1, 2), ("there", 2, 2), ("video", 2), ("read",), ("there", 0, 3), ("there", 1, 3),
    ("there", 2, 3), ("there", 0, 4), ("there", 1, 4), ("there", 2, 4),
    ("compute", 0), ("compute", 1), ("compute", 2), ("edges", 0), ("edges", 1), ("edges", 2),
    ("back", 0, 4), ("back", 1, 4), ("back", 2, 4),
    ("back", 0, 3), ("back", 1, 3), ("back", 2, 3), ("back", 0, 2), ("back", 1, 2), ("back", 2, 2),
    ("own", 0), ("own", 1), ("own", 2), ("back", 0, 1), ("back", 1, 1), ("back", 2, 1), ("finish", 0), ("finish", 1), ("finish", 2),
)


def dev(c, x, z):
    return {"grp": c, "seq": x * NZ + z}


def enter(c, x, z):
    barrier = pltpu.get_barrier_semaphore()

    def greet(*where):
        pl.semaphore_signal(barrier, inc=1, device_id=dev(*where), device_id_type=MESH)

    peers = [(r, dz) for dz in (-1, 0, 1) for r in range(NX) if r or dz]
    for r, dz in peers:
        greet(c, (x + r) % NX, (z + dz + NZ) % NZ)

    @pl.when(c > 0)
    def _():
        greet(c - 1, x, z)

    @pl.when(c < NC - 1)
    def _():
        greet(c + 1, x, z)

    inner = jnp.logical_and(c > 0, c < NC - 1)
    pl.semaphore_wait(barrier, len(peers) + 1 + inner.astype(jnp.int32))


def remote(src, dst, send, recv, where):
    return pltpu.make_async_remote_copy(
        src_ref=src, dst_ref=dst, send_sem=send, recv_sem=recv, device_id=dev(*where), device_id_type=MESH
    )


def local(src, dst, sem):
    return pltpu.make_async_copy(src, dst, sem)


def at(rel):
    return NZ - 1 if abs(rel) == 4 else 2 * rel if rel >= 0 else -2 * rel - 1


def head_cols(x, h):
    return pl.ds(pl.multiple_of((x * HPD + h) * HDIM, HDIM), HDIM)


def nt(a, b):
    return lax.dot_general(a, b, (((1,), (1,)), ((), ())), preferred_element_type=jnp.float32)


def tn(a, b):
    return lax.dot_general(a, b, (((0,), (0,)), ((), ())), preferred_element_type=jnp.float32)


def nn(a, b):
    return lax.dot_general(a, b, (((1,), (0,)), ((), ())), preferred_element_type=jnp.float32)


def kernel(
    q, g, k, v, lists, out_q, out_k, out_v,
    kv0, kv1, kv2, qg0, qg1, qg2, dq0, dq1, dq2, part0, part1, part2, edge0, edge1, edge2,
    moving0, moving1, moving2, landed0, landed1, landed2, final0, final1, final2,
    pads, mine, lists_v, lists_s, runs, leaving, home0, home1, home2,
    sent, up_sent, down_sent, audio_sem, video_sem, ring_sem, spread_sem, edge_sem, sum_sem, out_sem, home_sem, list_sem,
):
    c, s = lax.axis_index("grp"), lax.axis_index("seq")
    x, z = s // NZ, s % NZ
    enter(c, x, z)
    audio, video, outs = (k, v), (q, g), (out_k, out_v)
    kv, qg, dq = (kv0, kv1, kv2), (qg0, qg1, qg2), (dq0, dq1, dq2)
    part, edge = (part0, part1, part2), (edge0, edge1, edge2)
    moving, landed, final = (moving0, moving1, moving2), (landed0, landed1, landed2), (final0, final1, final2)
    home = (home0, home1, home2)
    above, below = jnp.minimum(c + 1, NC - 1), jnp.maximum(c - 1, 0)
    has_above, has_below = c < NC - 1, c > 0
    AUDIO, VIDEO, LIST, RING, SUM, QUERY, HOME = (sent.at[i] for i in range(7))

    def awaited(ref, sem):
        local(ref, ref, sem).wait()

    def peers():
        return [(x + r) % NX for r in range(1, NX)]

    def along(sign, hops):
        return (c, x, (z + sign * hops + NZ) % NZ)

    def send_audio(h):
        for w in range(2):
            for dz in (1, -1, 0) if h < NEAR else (0,):
                for r in range(NX):
                    to = (x + r) % NX
                    source, target = audio[w].at[:, head_cols(to, h)], kv[h].at[w, 2 + x, at(-dz)]
                    if dz or r:
                        remote(source, target, AUDIO, audio_sem.at[h, at(dz)], (c, to, (z + dz + NZ) % NZ)).start()
                    else:
                        local(source, target, audio_sem.at[h, 0]).start()

    def audio_in(h, dz):
        awaited(kv[h].at[:, pl.ds(2, NX), at(-dz)], audio_sem.at[h, at(dz)])

    def send_video(h):
        for w in range(2):
            for to in peers():
                source, target = video[w].at[:, head_cols(to, h)], qg[h].at[w, x]
                remote(source, target, VIDEO, video_sem.at[h], (c, to, z)).start()
            local(video[w].at[:, head_cols(x, h)], qg[h].at[w, x], video_sem.at[h]).start()

    def onward(h, d, step):
        sign = 1 - 2 * d
        what = pl.ds(0, 2) if step < 3 else pl.ds(d, 1)
        source = kv[h].at[what, pl.ds(2, NX), at(-sign * step)]
        target = kv[h].at[what, pl.ds(2, NX), at(-sign * (step + 1))]
        return remote(source, target, RING, ring_sem.at[h, d, step], along(sign, 1))

    def spread(h, low, count):
        span = pl.ds(low, count)

        @pl.when(has_above)
        def _():
            source, target = kv[h].at[:, pl.ds(4, 2), span], kv[h].at[:, pl.ds(0, 2), span]
            remote(source, target, up_sent.at[0], spread_sem.at[h, 0], (above, x, z)).start()

        @pl.when(has_below)
        def _():
            source, target = kv[h].at[:, pl.ds(2, 2), span], kv[h].at[:, pl.ds(6, 2), span]
            remote(source, target, down_sent.at[0], spread_sem.at[h, 1], (below, x, z)).start()

    def ready(h):
        awaited(qg[h], video_sem.at[h])

        @pl.when(has_above)
        def _():
            awaited(kv[h].at[:, pl.ds(6, 2)], spread_sem.at[h, 1])

        @pl.when(has_below)
        def _():
            awaited(kv[h].at[:, pl.ds(0, 2)], spread_sem.at[h, 0])

    def there(h, step):
        if step == 0:
            audio_in(h, 0)
        for d in range(2):
            if step == 0:
                onward(h, d, 0).start()
                continue
            if step == 1 and h < NEAR:
                audio_in(h, 1 - 2 * d)
            else:
                onward(h, d, step - 1).wait_recv()
            if step < 4:
                onward(h, d, step).start()
        if step == 2 and h < NEAR:
            audio_in(h, 0)
        if step > 1:
            spread(h, *SPREADS[step - 2])

    def send_lists():
        mine[...] = jnp.zeros_like(mine)
        mine[0:2, 0:LMAX] = lists[...]
        for to in peers():
            remote(mine, lists_v.at[x], LIST, list_sem.at[0], (c, to, z)).start()
        local(mine, lists_v.at[x], list_sem.at[0]).start()

    def clear():
        pads[:, :, 0:LMAX] = jnp.zeros((TILES, 2, LMAX, ROWS, HDIM), jnp.float32)
        pads[:, :, 2 * LMAX : 3 * LMAX] = jnp.zeros((TILES, 2, LMAX, ROWS, HDIM), jnp.float32)
        for h in range(HPD):

            @pl.when(c == 0)
            def _():
                edge[h][:, 0] = jnp.zeros((2,) + edge[h].shape[2:], BF16)

            @pl.when(c == NC - 1)
            def _():
                edge[h][:, 1] = jnp.zeros((2,) + edge[h].shape[2:], BF16)

    def read_lists():
        awaited(lists_v, list_sem.at[0])
        fetched = local(lists_v, lists_s, list_sem.at[1])
        fetched.start()
        fetched.wait()
        for t in range(TILES):
            count = jnp.int32(0)
            for j in range(LMAX):
                count += (lists_s[t // 2, t % 2, j] >= 0).astype(jnp.int32)
            runs[0, t] = jnp.clip(lists_s[t // 2, t % 2, 0] - (c * NX * NZ - NX * NZ // 2), 0, WIN - 1)
            runs[1, t] = count

    scale = HDIM**-0.5

    def tiles(h):
        loaded, ready_terms = [], []
        for t in range(TILES):
            first, count = runs[0, t], runs[1, t]
            blocks = [jnp.minimum(first + jnp.where(j < count, j, 0), WIN - 1) for j in range(LMAX)]
            places = [(e >> 3, ((e & 7) - z + NZ) & 7) for e in blocks]
            places = [(line, jnp.where(rel < 4, 2 * rel, 15 - 2 * rel)) for line, rel in places]
            kt = jnp.concatenate([kv[h][0, line, where] for line, where in places], axis=0)
            vt = jnp.concatenate([kv[h][1, line, where] for line, where in places], axis=0)
            rows = pl.ds(t % 2 * VBLK, VBLK)
            qt, gt = qg[h][0, t // 2, rows], qg[h][1, t // 2, rows]
            loaded.append((count, kt, qt, gt, nt(kt, qt), nt(vt, gt)))
        for count, kt, qt, gt, products, grad_weights in loaded:
            dead = [jnp.full((ROWS, VBLK), jnp.where(j < count, 0.0, MASKED), jnp.float32) for j in range(LMAX)]
            scores = products * (scale * LOG2E) + jnp.concatenate(dead, axis=0)
            raw = jnp.exp2(scores - jnp.max(scores, axis=0, keepdims=True))
            inverse = 1.0 / jnp.sum(raw, axis=0, keepdims=True)
            inner = jnp.sum(raw * grad_weights, axis=0, keepdims=True) * inverse
            weights_low = (raw * inverse).astype(BF16)
            grad_scores = (raw * ((grad_weights - inner) * (inverse * scale))).astype(BF16)
            ready_terms.append((kt, qt, gt, weights_low, grad_scores))
        for t, (kt, qt, gt, weights_low, grad_scores) in enumerate(ready_terms):
            pads[t, 1, LMAX : 2 * LMAX] = nn(weights_low, gt).reshape(LMAX, ROWS, HDIM)
            pads[t, 0, LMAX : 2 * LMAX] = nn(grad_scores, qt).reshape(LMAX, ROWS, HDIM)
            dq[h][t // 2, pl.ds(t % 2 * VBLK, VBLK)] = tn(grad_scores, kt).astype(BF16)

    def place(h):
        for w in range(2):
            for line in range(2 * NX):
                near = range(max(0, line - NX) * 2, min(NX, line + 1) * 2)
                total = None
                for t in near:
                    term = pads[t, w, pl.ds(jnp.clip(line * NZ - runs[0, t] + LMAX, 0, 2 * LMAX), LMAX)]
                    total = term if total is None else total + term
                total = total.astype(BF16)
                for zz in range(NZ):
                    rel = (zz - z + NZ) & 7
                    part[h][w, line, jnp.where(rel < 4, 2 * rel, 15 - 2 * rel)] = total[zz]

    def edge_copy(h, d, part_of):
        low, count = EDGES[part_of]
        line, to, sem = ((6, above, up_sent), (0, below, down_sent))[d]
        source, target = part[h].at[:, pl.ds(line, 2), pl.ds(low, count)], edge[h].at[:, d, :, pl.ds(low, count)]
        return remote(source, target, sem.at[1], edge_sem.at[h, d, part_of], (to, x, z))

    def send_edges(h, part_of):
        @pl.when(has_above)
        def _():
            edge_copy(h, 0, part_of).start()

        @pl.when(has_below)
        def _():
            edge_copy(h, 1, part_of).start()

    def send_queries(h):
        for to in peers():
            remote(dq[h].at[to], out_q.at[:, head_cols(x, h)], QUERY, out_sem.at[2], (c, to, z)).start()
        local(dq[h].at[x], out_q.at[:, head_cols(x, h)], out_sem.at[2]).start()

    def edges_in(h, part_of):
        @pl.when(has_above)
        def _():
            edge_copy(h, 1, part_of).wait_recv()

        @pl.when(has_below)
        def _():
            edge_copy(h, 0, part_of).wait_recv()

    def total(h, w, rel):
        p = at(rel)
        low = part[h][w, 2:4, p].astype(jnp.float32) + edge[h][w, 0, :, p].astype(jnp.float32)
        high = part[h][w, 4:6, p].astype(jnp.float32) + edge[h][w, 1, :, p].astype(jnp.float32)
        return jnp.concatenate([low, high], axis=0)

    def sum_copy(h, d, dist):
        what = pl.ds(0, 2) if dist < 4 else pl.ds(d, 1)
        source, target = moving[h].at[d, dist - 2, what], landed[h].at[d, dist - 2, what]
        return remote(source, target, SUM, sum_sem.at[h, d, dist - 2], along(1 - 2 * d, 1))

    def send_home(h, w, rel, value):
        leaving[h, w, at(rel)] = value.astype(BF16)
        for r in range(NX):
            to = (x + r) % NX
            source, target = leaving.at[h, w, at(rel), to], home[h].at[w, x, at(-rel)]
            if rel or r:
                remote(source, target, HOME, home_sem.at[h], (c, to, (z + rel + NZ) % NZ)).start()
            else:
                local(source, target, home_sem.at[h]).start()

    def back(h, dist):
        if dist > 1:
            edges_in(h, 4 - dist)
        for d in range(2):
            if dist < 4:
                sum_copy(h, d, dist + 1).wait_recv()
            for w in range(2):
                if dist == 4 and w != d:
                    continue
                value = total(h, w, -dist if d else dist)
                if dist < 3 or (dist == 3 and w == d):
                    value = value + landed[h][d, dist - 1, w].astype(jnp.float32)
                if dist == 1:
                    send_home(h, w, 1 - 2 * d, value)
                else:
                    moving[h][d, dist - 2, w] = value.astype(BF16)
            if dist > 1:
                sum_copy(h, d, dist).start()

    def own(h):
        for w in range(2):
            send_home(h, w, 0, total(h, w, 0))

    def finish(h):
        awaited(home[h], home_sem.at[h])
        for w in range(2):
            value = home[h][w, :, 0].astype(jnp.float32)
            for i in range(1, 3):
                value = value + home[h][w, :, i].astype(jnp.float32)
            final[h][w] = value.astype(BF16)
            for line in range(NX):
                local(final[h].at[w, line], outs[w].at[:, head_cols(line, h)], out_sem.at[w]).start()

    def compute(h):
        ready(h)
        tiles(h)
        place(h)
        send_edges(h, 0)
        send_edges(h, 1)
        send_queries(h)

    def edges(h):
        send_edges(h, 2)

    for action, *arguments in SCHEDULE:
        {
            "audio": send_audio, "video": send_video, "lists": send_lists, "clear": clear, "read": read_lists,
            "there": there, "compute": compute, "edges": edges, "back": back, "own": own, "finish": finish,
        }[action](*arguments)

    awaited(out_q, out_sem.at[2])
    for w in range(2):
        awaited(outs[w], out_sem.at[w])
    for i in range(2):

        @pl.when(has_above)
        def _():
            awaited(pads.at[pl.ds(0, 2), 0], up_sent.at[i])

        @pl.when(has_below)
        def _():
            awaited(pads.at[pl.ds(0, 2), 0], down_sent.at[i])

    for sem, a, b in ((AUDIO, 1, 17), (VIDEO, 3, 24), (RING, 4, 19), (SUM, 3, 20), (QUERY, 3, 12), (HOME, 3, 11)):
        awaited(pads.at[pl.ds(0, a), 0, pl.ds(0, b)], sem)
    awaited(lists_v.at[pl.ds(0, NX - 1)], LIST)


def copy_kernel(q, k, v, out_q, out_k, out_v, held_q, held_k, held_v, sem):
    half = VROWS // 2
    low, high = pl.ds(0, half), pl.ds(half, half)
    ways = (
        (q.at[low], held_q.at[low], out_q.at[low]), (q.at[high], held_q.at[high], out_q.at[high]),
        (k, held_k, out_k), (v, held_v, out_v),
    )
    first = [local(a, b, sem.at[0, i]) for i, (a, b, _) in enumerate(ways)]
    second = [local(b, o, sem.at[1, i]) for i, (_, b, o) in enumerate(ways)]
    for copy in first:
        copy.start()
    for one, two in zip(first, second):
        one.wait()
        two.start()
    for copy in second:
        copy.wait()


HBM = pl.BlockSpec(memory_space=pltpu.HBM)
VMEM = pl.BlockSpec(memory_space=pltpu.VMEM)


def sems(*shape):
    return pltpu.SemaphoreType.DMA(shape)


def each(*shape):
    return [pltpu.VMEM(shape, BF16)] * HPD


def per_device(q, k, v, g, lists):
    grads = pl.pallas_call(
        kernel,
        out_shape=tuple(jax.ShapeDtypeStruct(a.shape, BF16) for a in (q, k, v)),
        in_specs=[HBM] * 4 + [VMEM],
        out_specs=(HBM,) * 3,
        scratch_shapes=[
            *each(2, 2 * NX, NZ, ROWS, HDIM),
            *each(2, NX, VROWS, HDIM),
            *each(NX, VROWS, HDIM),
            *each(2, 2 * NX, NZ, ROWS, HDIM),
            *each(2, 2, 2, NZ, ROWS, HDIM),
            *each(2, 3, 2, NX, ROWS, HDIM),
            *each(2, 3, 2, NX, ROWS, HDIM),
            *each(2, NX, ROWS, HDIM),
            pltpu.VMEM((TILES, 2, 3 * LMAX, ROWS, HDIM), jnp.float32),
            pltpu.VMEM((8, 128), jnp.int32),
            pltpu.VMEM((NX, 8, 128), jnp.int32),
            pltpu.SMEM((NX, 8, 128), jnp.int32),
            pltpu.SMEM((2, TILES), jnp.int32),
            pltpu.VMEM((HPD, 2, 3, NX, ROWS, HDIM), BF16),
            *each(2, NX, 3, ROWS, HDIM),
            sems(7), sems(2), sems(2), sems(HPD, 3), sems(HPD), sems(HPD, 2, 4), sems(HPD, 2),
            sems(HPD, 2, len(EDGES)), sems(HPD, 2, 3), sems(3), sems(HPD), sems(2),
        ],
        compiler_params=pltpu.CompilerParams(
            collective_id=0, has_side_effects=True, vmem_limit_bytes=62 * 2**20
        ),
        name="cross_attention_backward",
    )(q, g, k, v, lists)
    return pl.pallas_call(
        copy_kernel,
        out_shape=tuple(jax.ShapeDtypeStruct(a.shape, BF16) for a in (q, k, v)),
        in_specs=[HBM] * 3,
        out_specs=(HBM,) * 3,
        scratch_shapes=[*(pltpu.VMEM(a.shape, BF16) for a in (q, k, v)), sems(2, 4)],
        name="final_copies",
    )(*grads)


def solution(mesh):
    placed = P(("grp", "seq"), None)
    return jax.shard_map(
        per_device,
        mesh=mesh,
        in_specs=(placed,) * 5,
        out_specs=(placed,) * 3,
        check_vma=False,
    )
```
